32 devices in a mesh: tiles: 2 (over x), disp: 8 (over z, y), rows: 2 (over core).
Axes of the slice: x: 2, y: 2, z: 4, core: 2. Of those that a mesh axis runs over, the one named last changes fastest.
Arguments:
- volume: bfloat16 [32, 192, 64, 512], P(None, 'disp', ('tiles', 'rows')), parts along dimension 2, may hold values from -1000 to 1000, as said below
- conv_weight: bfloat16 [27, 32, 32], replicated, may hold values from -0.21875 to 0.21875
- conv_bias: float32 [32], replicated, may hold values from -3 to 3
- reg_weight: bfloat16 [27, 32], replicated, may hold values from -0.875 to 0.875
Outputs:
- disparity: float32 [64, 512], P(('tiles', 'rows')), parts along dimension 0
The draws below stay inside these ranges and needn't reach their ends.
There are 2 independent parts, one for each index of `tiles`. The reference program is written for one: setup_inputs(seed, part) draws one part's arguments, and reference() takes and returns one part's arrays. A program takes and returns all parts, laid end to end along the dimension named above; an argument that names none is the same for every part. Nothing has to cross between parts.
Inputs may be any that keep to these rules, and one draw needn't show every extreme that they name: `volume`: Real-valued matching features.
All inputs are finite; a program needn't handle non-finite values.
Results may differ from the reference program's by a relative error of at most 0.008.
Values may be sent and summed in bfloat16 or wider, within the bound.
No kernel may reach another device: no remote copies, remote signals or barrier semaphores. Data moves between devices by JAX's collectives and lax.ppermute only.
A program may use at most 384 MiB of HBM per device.

```python
import jax
import jax.numpy as jnp
from jax import lax

CH = 32
DISP = 192
WIDTH = 512
ROWS = 32


def draw_volume(key, part):
    first = jax.random.fold_in(jax.random.fold_in(key, 7), 0)
    base = jnp.clip(jax.random.normal(first, (CH, DISP, ROWS, WIDTH), jnp.float32), -6.0, 6.0)
    return base.astype(jnp.bfloat16)


def bell_draw(key, dims, deviation, limit, held_as=jnp.bfloat16):
    drawn = deviation * jax.random.normal(key, dims, jnp.float32)
    return jnp.clip(drawn, min=-limit, max=limit).astype(held_as)


def setup_inputs(seed: int = 0, part: int = 0) -> dict:
    splits = jax.random.split(jax.random.key(seed), 5)
    part_splits = jax.random.split(jax.random.fold_in(splits[4], part), 5)
    volume = draw_volume(jax.random.fold_in(jax.random.fold_in(splits[4], part), 71), part)
    conv_weight = bell_draw(splits[1], (27, CH, CH), (27 * CH) ** -0.5, 0.21875)
    conv_bias = bell_draw(splits[2], (CH,), 0.5, 3.0, jnp.float32)
    reg_weight = bell_draw(splits[3], (27, CH), (27 * CH // 16) ** -0.5, 0.875)
    return {"volume": volume, "conv_weight": conv_weight, "conv_bias": conv_bias, "reg_weight": reg_weight}


def aggregate(volume, conv_weight, conv_bias):
    padded = jnp.pad(volume, ((0, 0), (1, 1), (1, 1), (1, 1))).astype(jnp.float32)
    weights = conv_weight.astype(jnp.float32)
    summed = jnp.zeros((CH, DISP, ROWS, WIDTH), jnp.float32)
    for depth_tap in range(3):
        for row_tap in range(3):
            for col_tap in range(3):
                window = padded[:, depth_tap:depth_tap + DISP, row_tap:row_tap + ROWS, col_tap:col_tap + WIDTH]
                summed = summed + jnp.einsum("oc,cdhw->odhw", weights[9 * depth_tap + 3 * row_tap + col_tap], window, precision=lax.Precision.HIGHEST)
    return jnp.maximum(summed + conv_bias[:, None, None, None], 0.0).astype(jnp.bfloat16)


def regress(hidden, reg_weight):
    padded = jnp.pad(hidden, ((0, 0), (1, 1), (1, 1), (1, 1))).astype(jnp.float32)
    weights = reg_weight.astype(jnp.float32)
    cost = jnp.zeros((DISP, ROWS, WIDTH), jnp.float32)
    for depth_tap in range(3):
        for row_tap in range(3):
            for col_tap in range(3):
                window = padded[:, depth_tap:depth_tap + DISP, row_tap:row_tap + ROWS, col_tap:col_tap + WIDTH]
                cost = cost + jnp.einsum("c,cdhw->dhw", weights[9 * depth_tap + 3 * row_tap + col_tap], window, precision=lax.Precision.HIGHEST)
    return cost


def reference(volume, conv_weight, conv_bias, reg_weight):
    hidden = aggregate(volume, conv_weight, conv_bias)
    cost = regress(hidden, reg_weight)
    score = -cost
    peak = jnp.max(score, axis=0)
    expo = jnp.exp(score - peak[None])
    planes = jnp.arange(DISP).astype(jnp.float32)
    total = jnp.sum(expo, axis=0)
    moment = jnp.sum(planes[:, None, None] * expo, axis=0)
    return moment / total
```

```python
import functools

import jax
import jax.numpy as jnp
import numpy as np
from jax import lax
from jax.experimental import pallas as pl
from jax.experimental.pallas import tpu as pltpu
from jax.sharding import PartitionSpec as P

BF16 = jnp.bfloat16
F32 = jnp.float32
LANES = 256

PAIR = (
    (((0, 1, 0, 3), (0, 2, 0, 3), (0, 0, 0, 2)), ((0, 0), (0, 1))),
    (((3, 1, 0, 3), (3, 2, 0, 3), (3, 3, 0, 2)), ((1, 0), (1, 1))),
    (((1, 0, 0, 3), (2, 0, 0, 3), (3, 0, 0, 2)), ((0, 0), (1, 0))),
    (((1, 3, 0, 3), (2, 3, 0, 3), (0, 3, 0, 2)), ((0, 1), (1, 1))),
    (((1, 1, 0, 3), (1, 2, 0, 3), (0, 0, 2, 3), (0, 3, 2, 3)), ((0, 0), (0, 1), (1, 0), (1, 1))),
    (((2, 1, 0, 3), (2, 2, 0, 3), (3, 3, 2, 3), (3, 0, 2, 3)), ((0, 0), (0, 1), (1, 0), (1, 1))),
)
SINGLE = (
    (((0, 0, 0, 3), (1, 0, 0, 3), (2, 0, 0, 2)), ((0, 0),)),
    (((0, 3, 0, 3), (1, 3, 0, 3), (2, 3, 0, 2)), ((0, 1),)),
    (((0, 1, 0, 3), (0, 2, 0, 3), (1, 1, 0, 2)), ((0, 0), (0, 1))),
    (((1, 1, 2, 3), (1, 2, 0, 3), (2, 1, 0, 3), (2, 2, 0, 1)), ((0, 0), (0, 1))),
    (((2, 2, 1, 3), (2, 0, 2, 3), (2, 3, 2, 3)), ((0, 0), (0, 1))),
)


def tap_table(spec):
    rows = []
    for blocks, outs in spec:
        for do, ho in outs:
            row = []
            for dd, hh, c0, c1 in blocks:
                for c in range(c0, c1):
                    a, b = dd - do, hh - ho
                    row.append(9 * a + 3 * b + c if 0 <= a < 3 and 0 <= b < 3 else 27)
            rows.append(row + [27] * (8 - len(row)))
    return np.array(rows)


def packed_weights(conv_weight, spec):
    table = tap_table(spec)
    pick = jnp.asarray(table[:, :, None] == np.arange(27), BF16)
    ch = conv_weight.shape[1]
    out = jnp.einsum("mkt,toi->moki", pick, conv_weight, preferred_element_type=F32)
    return out.astype(BF16).reshape(table.shape[0] * ch, 8 * ch)


def regression_rows(reg_weight, rows, inputs, first):
    ch = reg_weight.shape[1]
    taps = reg_weight.reshape(3, 3, 3, ch)
    total = None
    for b in range(3):
        hit = np.arange(inputs)[None, :] + first == np.arange(rows)[:, None] + b - 1
        hit = jnp.asarray(hit, BF16)
        term = taps[:, b][:, :, None, None, :] * hit[None, None, :, :, None]
        total = term if total is None else total + term
    return total.reshape(9 * rows, inputs * ch)


def edge_rows(reg_weight, rows):
    ch = reg_weight.shape[1]
    taps = reg_weight.reshape(3, 3, 3, ch)
    before = jnp.pad(taps[:, 2], ((0, 0), (0, 0), (0, (rows - 1) * ch)))
    after = jnp.pad(taps[:, 0], ((0, 0), (0, 0), ((rows - 1) * ch, 0)))
    both = jnp.concatenate([before, after, jnp.zeros((3, 2, rows * ch), BF16)], axis=1)
    return both.reshape(24, rows * ch)


def shifted(x, by):
    width = x.shape[-1]
    moved = pltpu.roll(x, by % width, x.ndim - 1)
    lane = lax.broadcasted_iota(jnp.int32, x.shape[:-1] + (128,), x.ndim - 1)
    zero = jnp.zeros(x.shape[:-1] + (128,), x.dtype)
    if by == 1:
        edge = jnp.where(lane == 0, zero, moved[..., :128])
        return jnp.concatenate([edge, moved[..., 128:]], axis=-1)
    edge = jnp.where(lane == 127, zero, moved[..., width - 128 :])
    return jnp.concatenate([moved[..., : width - 128], edge], axis=-1)


def put(taps_ref, slot, row, count, at, x):
    size, width = x.shape[1], x.shape[2]
    ch = taps_ref.shape[2] // 3
    flat = x.reshape(count * size, width)
    for c, y in ((0, shifted(flat, 1)), (1, flat), (2, shifted(flat, -1))):
        where = pl.ds(c * ch + at, size)
        taps_ref[slot, pl.ds(row, count), where, :] = y.reshape(count, size, width)


def stage(taps_ref, slot, first_row, block, half):
    size = block.shape[0]
    put(taps_ref, slot, first_row, block.shape[1], half * size, jnp.swapaxes(block, 0, 1))


def patch(spec, taps_ref, slots, row, lanes, weight_ref):
    ch = taps_ref.shape[2] // 3
    sums = {}
    at = 0
    for blocks, outs in spec:
        pieces = [
            taps_ref[slots[dd], row + hh, c0 * ch : c1 * ch, lanes] for dd, hh, c0, c1 in blocks
        ]
        x = jnp.concatenate(pieces, axis=0)
        w = weight_ref[at : at + len(outs) * ch, : x.shape[0]]
        y = jnp.dot(w, x, preferred_element_type=F32)
        for k, out in enumerate(outs):
            part = y[k * ch : (k + 1) * ch]
            sums[out] = part if out not in sums else sums[out] + part
        at += len(outs) * ch
    return sums


def inner_kernel(
    vol_ref, above_ref, below_ref, weight_ref, bias_ref, reg_ref, cost_ref, edge_ref,
    taps_ref, hidden_ref, acc_ref, acc_edge_ref,
):
    s = pl.program_id(0)
    last = pl.num_programs(0) - 1
    ch, _, rows, width = vol_ref.shape
    planes = cost_ref.shape[0]
    half = ch // 2
    new = (s % 3) * 2

    def stage_part(part):
        p, h = part // 2, part % 2
        if h == 0:
            put(taps_ref, new + p, 0, 1, 0, above_ref[p][None])
            put(taps_ref, new + p, rows + 1, 1, 0, below_ref[p][None])
        block = vol_ref[h * half : (h + 1) * half, p]
        stage(taps_ref, new + p, 1, block, h)

    @pl.when(s < 2)
    def _():
        for part in range(4):
            stage_part(part)

    @pl.when(s == 2)
    def _():
        acc_ref[...] = jnp.zeros_like(acc_ref)
        acc_edge_ref[...] = jnp.zeros_like(acc_edge_ref)

    @pl.when(s >= 2)
    def _():
        old = ((s - 2) % 3) * 2
        mid = ((s - 1) % 3) * 2
        slots = (old, old + 1, mid, mid + 1)
        pairs = rows // 2
        done = 0
        for j in range(pairs):
            for n in range(0, width, LANES):
                lanes = slice(n, n + LANES)
                sums = patch(PAIR, taps_ref, slots, 2 * j, lanes, weight_ref)
                for (do, ho), y in sums.items():
                    y = jnp.maximum(y + bias_ref[...], 0.0).astype(BF16)
                    at = (2 * j + ho) * ch
                    hidden_ref[do, at : at + ch, lanes] = y
            while done * pairs < 4 * (j + 1) and done < 4:
                stage_part(done)
                done += 1
        first = 2 * (s - 2) + 1
        for do in range(2):
            for n in range(0, width, LANES):
                lanes = slice(n, n + LANES)
                y = jnp.dot(reg_ref[...], hidden_ref[do, :, lanes], preferred_element_type=F32)
                for a in range(3):
                    plane = first + do + 1 - a
                    for c in range(3):
                        at = (a * 3 + c) * rows
                        acc_ref[c, plane, :, lanes] += y[at : at + rows]
                    at = 9 * rows + a * 8
                    acc_edge_ref[plane, :, lanes] += y[at : at + 8]

    @pl.when(s == last)
    def _():
        def finish(d, carry):
            cost_ref[d] = shifted(acc_ref[0, d], 1) + acc_ref[1, d] + shifted(acc_ref[2, d], -1)
            e = acc_edge_ref[d]
            right, left = shifted(e, 1), shifted(e, -1)
            edge_ref[0, pl.ds(d, 1)] = right[0:1] + e[1:2] + left[2:3]
            edge_ref[1, pl.ds(d, 1)] = right[3:4] + e[4:5] + left[5:6]
            return carry

        lax.fori_loop(0, planes, finish, 0)


def inner(volume, above, below, weights, bias, reg):
    ch, planes, rows, width = volume.shape
    blocks = planes // 2
    block = lambda s: jnp.minimum(s, blocks - 1)
    whole = lambda x: pl.BlockSpec(x.shape, lambda s: (0,) * x.ndim)
    cost = jax.ShapeDtypeStruct((planes, rows, width), F32)
    edge = jax.ShapeDtypeStruct((2, planes, width), F32)
    work = 2 * 27 * ch * ch * planes * rows * width
    return pl.pallas_call(
        inner_kernel,
        name="inner",
        grid=(blocks + 1,),
        out_shape=(cost, edge),
        in_specs=[
            pl.BlockSpec((ch, 2, rows, width), lambda s: (0, block(s), 0, 0)),
            pl.BlockSpec((2, ch, width), lambda s: (block(s), 0, 0)),
            pl.BlockSpec((2, ch, width), lambda s: (block(s), 0, 0)),
            whole(weights), whole(bias), whole(reg),
        ],
        out_specs=(
            pl.BlockSpec(cost.shape, lambda s: (0, 0, 0)),
            pl.BlockSpec(edge.shape, lambda s: (0, 0, 0)),
        ),
        scratch_shapes=[
            pltpu.VMEM((6, rows + 2, 3 * ch, width), BF16),
            pltpu.VMEM((2, rows * ch, width), BF16),
            pltpu.VMEM((3, planes, rows, width), F32),
            pltpu.VMEM((planes, 8, width), F32),
        ],
        compiler_params=pltpu.CompilerParams(vmem_limit_bytes=40 << 20),
        cost_estimate=pl.CostEstimate(
            flops=2 * work, bytes_accessed=volume.size * 2, transcendentals=0
        ),
    )(volume, above, below, weights, bias, reg)


def outer_kernel(
    keep_ref, vol_ref, lo_ref, hi_ref, above_ref, below_ref, weight_ref, bias_ref, reg_ref, out_ref,
    taps_ref, hidden_ref,
):
    s = pl.program_id(0)
    ch, _, rows, width = vol_ref.shape
    half = ch // 2
    for p in range(3):
        put(taps_ref, p, 0, 2, 0, above_ref[p])
        put(taps_ref, p, rows + 2, 2, 0, below_ref[p])
    for h in range(2):
        part = slice(h * half, (h + 1) * half)
        far = jnp.where(s == 0, lo_ref[part], hi_ref[part])
        stage(taps_ref, 2 * s, 2, far, h)
        for p in range(2):
            stage(taps_ref, 1 + p - s, 2, vol_ref[part, p], h)
    pairs = rows // 2 + 1
    for j in range(pairs):
        for n in range(0, width, LANES):
            lanes = slice(n, n + LANES)
            sums = patch(SINGLE, taps_ref, (0, 1, 2), 2 * j, lanes, weight_ref)
            for (_, ho), y in sums.items():
                y = jnp.maximum(y + bias_ref[...], 0.0)
                r = 2 * j + ho
                if r == 0:
                    y = jnp.where(keep_ref[0] > 0, y, 0.0)
                if r == rows + 1:
                    y = jnp.where(keep_ref[1] > 0, y, 0.0)
                hidden_ref[r * ch : (r + 1) * ch, lanes] = y.astype(BF16)
    y = jnp.dot(reg_ref[...], hidden_ref[...], preferred_element_type=F32)
    for a in range(3):
        r = [y[(a * 3 + c) * rows : (a * 3 + c + 1) * rows] for c in range(3)]
        out_ref[0, 2 - a] = shifted(r[0], 1) + r[1] + shifted(r[2], -1)


def outer(keep, volume, lo, hi, above, below, weights, bias, reg):
    ch, planes, rows, width = volume.shape
    whole = lambda x: pl.BlockSpec(x.shape, lambda s: (0,) * x.ndim)
    out = jax.ShapeDtypeStruct((2, 3, rows, width), F32)
    work = 2 * 27 * ch * ch * 2 * rows * width
    return pl.pallas_call(
        outer_kernel,
        name="outer",
        grid=(2,),
        out_shape=out,
        in_specs=[
            pl.BlockSpec(memory_space=pltpu.SMEM),
            pl.BlockSpec((ch, 2, rows, width), lambda s: (0, s * (planes // 2 - 1), 0, 0)),
            whole(lo), whole(hi),
            pl.BlockSpec((3, 2, ch, width), lambda s: (s, 0, 0, 0)),
            pl.BlockSpec((3, 2, ch, width), lambda s: (s, 0, 0, 0)),
            whole(weights), whole(bias), whole(reg),
        ],
        out_specs=pl.BlockSpec((1, 3, rows, width), lambda s: (s, 0, 0, 0)),
        scratch_shapes=[
            pltpu.VMEM((3, rows + 4, 3 * ch, width), BF16),
            pltpu.VMEM(((rows + 2) * ch, width), BF16),
        ],
        compiler_params=pltpu.CompilerParams(vmem_limit_bytes=40 << 20),
        cost_estimate=pl.CostEstimate(flops=2 * work, bytes_accessed=1 << 22, transcendentals=0),
    )(keep, volume, lo, hi, above, below, weights, bias, reg)


def stats_kernel(
    first_ref, cost_ref, above_ref, below_ref, outer_ref, lo_ref, hi_ref, out_ref, score_ref
):
    planes, rows, width = cost_ref.shape
    row = lax.broadcasted_iota(jnp.int32, (rows, width), 0)
    extra = {0: outer_ref[0, 1] + lo_ref[...], 1: outer_ref[0, 2]}
    for d, x in ((planes - 2, outer_ref[1, 0]), (planes - 1, outer_ref[1, 1] + hi_ref[...])):
        extra[d] = x if d not in extra else extra[d] + x
    peak = None
    for d in range(planes):
        cost = cost_ref[d]
        cost = cost + jnp.where(row == 0, above_ref[d : d + 1], 0.0)
        cost = cost + jnp.where(row == rows - 1, below_ref[d : d + 1], 0.0)
        if d in extra:
            cost = cost + extra[d]
        score = -cost
        score_ref[d] = score
        peak = score if peak is None else jnp.maximum(peak, score)
    total = jnp.zeros((rows, width), F32)
    moment = jnp.zeros((rows, width), F32)
    first = first_ref[0].astype(F32)
    for d in range(planes):
        expo = jnp.exp(score_ref[d] - peak)
        total = total + expo
        moment = moment + (first + float(d)) * expo
    out_ref[0] = peak
    out_ref[1] = total
    out_ref[2] = moment


def stats(first, cost, above, below, outer_out, lo, hi):
    planes, rows, width = cost.shape
    vmem = pl.BlockSpec(memory_space=pltpu.VMEM)
    return pl.pallas_call(
        stats_kernel,
        name="stats",
        out_shape=jax.ShapeDtypeStruct((3, rows, width), F32),
        in_specs=[pl.BlockSpec(memory_space=pltpu.SMEM)] + [vmem] * 6,
        out_specs=vmem,
        scratch_shapes=[pltpu.VMEM((planes, rows, width), F32)],
        compiler_params=pltpu.CompilerParams(vmem_limit_bytes=40 << 20),
    )(first, cost, above, below, outer_out, lo, hi)


def combine(first, second):
    peak = jnp.maximum(first[0], second[0])
    left = jnp.exp(first[0] - peak)
    right = jnp.exp(second[0] - peak)
    return jnp.stack(
        [peak, first[1] * left + second[1] * right, first[2] * left + second[2] * right]
    )


def up(x, axis):
    count = lax.axis_size(axis)
    return lax.ppermute(x, axis, [(i, i + 1) for i in range(count - 1)])


def down(x, axis):
    count = lax.axis_size(axis)
    return lax.ppermute(x, axis, [(i + 1, i) for i in range(count - 1)])


def joined(value, axis):
    count = lax.axis_size(axis)
    if count & (count - 1):
        pieces = lax.all_gather(value, axis)
        return functools.reduce(combine, [pieces[i] for i in range(count)])
    index = lax.axis_index(axis)
    step = 1
    while step < count:
        other = lax.ppermute(value, axis, [(i, i ^ step) for i in range(count)])
        lower = (index & step) == 0
        value = combine(jnp.where(lower, value, other), jnp.where(lower, other, value))
        step *= 2
    return value


def body(volume, conv_weight, conv_bias, reg_weight):
    ch, planes, rows, width = volume.shape
    bias = jnp.broadcast_to(conv_bias[:, None], (ch, LANES))
    pair_weights = packed_weights(conv_weight, PAIR)
    single_weights = packed_weights(conv_weight, SINGLE)
    reg_inner = jnp.concatenate(
        [regression_rows(reg_weight, rows, rows, 0), edge_rows(reg_weight, rows)], axis=0
    )
    reg_outer = regression_rows(reg_weight, rows, rows + 2, -1)

    top = jnp.transpose(volume[:, :, 0, :], (1, 0, 2))
    bottom = jnp.transpose(volume[:, :, rows - 1, :], (1, 0, 2))
    above = up(bottom, "rows")
    below = down(top, "rows")

    lo = up(volume[:, planes - 1], "disp")
    hi = down(volume[:, 0], "disp")
    ends = [lo, volume[:, 0], volume[:, 1], volume[:, planes - 2], volume[:, planes - 1], hi]
    turned = lambda r: jnp.stack([jnp.swapaxes(x[:, r : r + 2], 0, 1) for x in ends])
    above2 = up(turned(rows - 2), "rows")
    below2 = down(turned(0), "rows")

    cost, edge = inner(volume, above, below, pair_weights, bias, reg_inner)
    edge_above = up(edge[1], "rows")
    edge_below = down(edge[0], "rows")

    row_index = lax.axis_index("rows")
    keep = jnp.stack([row_index > 0, row_index < lax.axis_size("rows") - 1]).astype(jnp.int32)
    ends_cost = outer(keep, volume, lo, hi, above2, below2, single_weights, bias, reg_outer)
    from_lo = up(ends_cost[1, 2], "disp")
    from_hi = down(ends_cost[0, 0], "disp")

    first = (lax.axis_index("disp") * planes).astype(jnp.int32).reshape(1)
    value = stats(first, cost, edge_above, edge_below, ends_cost, from_lo, from_hi)
    _, total, moment = joined(value, "disp")
    return moment / total


def solution(mesh):
    in_specs = (P(None, "disp", ("tiles", "rows"), None), P(), P(), P())
    out_specs = P(("tiles", "rows"), None)
    return jax.shard_map(body, mesh=mesh, in_specs=in_specs, out_specs=out_specs, check_vma=False)
```

```python
import functools

import jax
import jax.numpy as jnp
import numpy as np
from jax import lax
from jax.experimental import pallas as pl
from jax.experimental.pallas import tpu as pltpu
from jax.sharding import PartitionSpec as P

BF16 = jnp.bfloat16
F32 = jnp.float32
LANES = 256
VMEM = pl.BlockSpec(memory_space=pltpu.VMEM)
SMEM = pl.BlockSpec(memory_space=pltpu.SMEM)
ROOM = pltpu.CompilerParams(vmem_limit_bytes=48 << 20)

SINGLE = (
    (((0, 0, 0, 3), (1, 0, 0, 3), (2, 0, 0, 2)), (0,)),
    (((0, 3, 0, 3), (1, 3, 0, 3), (2, 3, 0, 2)), (1,)),
    (((0, 1, 0, 3), (0, 2, 0, 3), (1, 1, 0, 2)), (0, 1)),
    (((1, 1, 2, 3), (1, 2, 0, 3), (2, 1, 0, 3), (2, 2, 0, 1)), (0, 1)),
    (((2, 2, 1, 3), (2, 0, 2, 3), (2, 3, 2, 3)), (0, 1)),
)


def tap(a, b, c):
    return 9 * a + 3 * b + c if 0 <= a < 3 and 0 <= b < 3 else None


def single_table():
    table = []
    for blocks, outs in SINGLE:
        for ho in outs:
            row = [tap(dd, hh - ho, c) for dd, hh, c0, c1 in blocks for c in range(c0, c1)]
            table.append(row + [None] * (8 - len(row)))
    return table


def spread_table():
    return [
        [tap(2 - do, hi - ho + 2, c) for hi in range(2) for c in range(3)]
        for ho in range(4) for do in range(3)
    ]


def halo_table(b):
    return [[tap(p - q + 2, b, c) for p in range(2) for c in range(3)] for q in range(4)]


def pack_kernel(tables, conv_ref, *out_refs):
    ch = conv_ref.shape[1]
    for table, out_ref in zip(tables, out_refs):
        for m, row in enumerate(table):
            for k, t in enumerate(row):
                block = jnp.zeros((ch, ch), BF16) if t is None else conv_ref[t]
                out_ref[m * ch : (m + 1) * ch, k * ch : (k + 1) * ch] = block


def packed(conv_weight):
    ch = conv_weight.shape[1]
    tables = [spread_table(), halo_table(0), halo_table(2), single_table()]
    outs = [jax.ShapeDtypeStruct((len(t) * ch, len(t[0]) * ch), BF16) for t in tables]
    return pl.pallas_call(
        functools.partial(pack_kernel, tables),
        name="pack",
        out_shape=outs,
        in_specs=[VMEM],
        out_specs=[VMEM] * len(outs),
        compiler_params=ROOM,
    )(conv_weight)


def regression_rows(reg_weight, rows, inputs, first):
    ch = reg_weight.shape[1]
    taps = reg_weight.reshape(3, 3, 3, ch)
    total = None
    for b in range(3):
        hit = np.arange(inputs)[None, :] + first == np.arange(rows)[:, None] + b - 1
        hit = jnp.asarray(hit, BF16)
        term = taps[:, b][:, :, None, None, :] * hit[None, None, :, :, None]
        total = term if total is None else total + term
    return total.reshape(9 * rows, inputs * ch)


def regression_edges(reg_weight, rows):
    ch = reg_weight.shape[1]
    pick = np.zeros((4, 24, 2, 2, 27))
    for q in range(4):
        for p in range(2):
            for c in range(3):
                for k, out in enumerate((-1, 0, 1, rows - 2, rows - 1, rows)):
                    for e, row in enumerate((0, rows - 1)):
                        t = tap(p - q + 2, row - out + 1, c)
                        if t is not None:
                            pick[q, c * 6 + k, p, e, t] = 1
    pick = jnp.asarray(pick.reshape(96, 4, 27), BF16)
    out = jnp.einsum("mkt,ti->mki", pick, reg_weight, preferred_element_type=F32)
    return out.astype(BF16).reshape(96, 4 * ch)


def shifted(x, by):
    width = x.shape[-1]
    moved = pltpu.roll(x, by % width, x.ndim - 1)
    lane = lax.broadcasted_iota(jnp.int32, x.shape[:-1] + (128,), x.ndim - 1)
    zero = jnp.zeros(x.shape[:-1] + (128,), x.dtype)
    if by == 1:
        edge = jnp.where(lane == 0, zero, moved[..., :128])
        return jnp.concatenate([edge, moved[..., 128:]], axis=-1)
    edge = jnp.where(lane == 127, zero, moved[..., width - 128 :])
    return jnp.concatenate([moved[..., : width - 128], edge], axis=-1)


def put(taps_ref, slot, row, at, x):
    count, size, width = x.shape
    ch = taps_ref.shape[2] // 3
    flat = x.reshape(count * size, width)
    for c, y in ((0, shifted(flat, 1)), (1, flat), (2, shifted(flat, -1))):
        taps_ref[slot, pl.ds(row, count), pl.ds(c * ch + at, size), :] = y.reshape(x.shape)


def edges_kernel(side_ref, vol_ref, near_ref, first_ref, last_ref):
    s = pl.program_id(0)
    steps = pl.num_programs(0)
    rows = vol_ref.shape[2]
    planes = 2 * steps
    top = side_ref[0] == 0
    for p in range(2):
        row = jnp.where(top, vol_ref[:, p, rows - 1, :], vol_ref[:, p, 0, :])
        near_ref[2 * s + p] = row

    @pl.when((s == 0) | (s == steps - 1))
    def _():
        for p in range(2):
            row = jnp.where(top, vol_ref[:, p, rows - 2, :], vol_ref[:, p, 1, :])
            near_ref[planes + p + jnp.where(s == 0, 0, 2)] = row

    @pl.when(s == 0)
    def _():
        first_ref[...] = jnp.swapaxes(vol_ref[:, 0], 0, 1)

    @pl.when(s == steps - 1)
    def _():
        last_ref[...] = jnp.swapaxes(vol_ref[:, 1], 0, 1)


def edges(side, volume):
    ch, planes, rows, width = volume.shape
    near = jax.ShapeDtypeStruct((planes + 4, ch, width), BF16)
    plane = jax.ShapeDtypeStruct((rows, ch, width), BF16)
    zero = lambda s: (0, 0, 0)
    return pl.pallas_call(
        edges_kernel,
        name="edges",
        grid=(planes // 2,),
        out_shape=(near, plane, plane),
        in_specs=[SMEM, pl.BlockSpec((ch, 2, rows, width), lambda s: (0, s, 0, 0))],
        out_specs=[pl.BlockSpec(x.shape, zero) for x in (near, plane, plane)],
        compiler_params=ROOM,
    )(side, volume)


def inner_kernel(
    vol_ref, weight_ref, bias_ref, reg_ref, cost_ref, pre_ref,
    taps_ref, acc_ref, hidden_ref, sums_ref,
):
    s = pl.program_id(0)
    last = pl.num_programs(0) - 1
    ch, _, rows, width = vol_ref.shape
    planes = cost_ref.shape[0]
    half = ch // 2
    new = (s % 2) * 2
    old = ((s + 1) % 2) * 2

    def stage(part):
        p, h = part // 2, part % 2
        block = vol_ref[h * half : (h + 1) * half, p]
        put(taps_ref, new + p, 0, h * half, jnp.swapaxes(block, 0, 1))

    @pl.when(s == 0)
    def _():
        for part in range(4):
            stage(part)
        sums_ref[...] = jnp.zeros_like(sums_ref)
        hidden_ref[...] = jnp.zeros_like(hidden_ref)

    @pl.when(s >= 1)
    def _():
        base = 2 * (s - 1) + 3
        tiles = rows // 2
        for p in range(2):
            slots = [(base + p + do) % 4 for do in range(3)]
            for j in range(tiles):
                ho0 = 1 if j == 0 else 0
                ho1 = 3 if j == tiles - 1 else 4
                w = weight_ref[ho0 * 3 * ch : ho1 * 3 * ch]
                for n in range(0, width, LANES):
                    lanes = slice(n, n + LANES)
                    x = taps_ref[old + p, 2 * j : 2 * j + 2, :, lanes].reshape(6 * ch, LANES)
                    y = jnp.dot(w, x, preferred_element_type=F32)
                    for ho in range(ho0, ho1):
                        for do in range(3):
                            at = ((ho - ho0) * 3 + do) * ch
                            part = y[at : at + ch]
                            fresh = do == 2 and (ho >= 2 or j == 0)
                            if not fresh:
                                part = part + acc_ref[slots[do], 2 * j + ho, :, lanes]
                            acc_ref[slots[do], 2 * j + ho, :, lanes] = part
                if j % (tiles // 2) == tiles // 2 - 1:
                    stage(2 * p + j // (tiles // 2))

    @pl.when(s >= 2)
    def _():
        first = 2 * (s - 1) - 1
        for q in range(2):
            slot = (first + q) % 4
            pre_ref[q, 0] = acc_ref[slot, 1]
            pre_ref[q, 1] = acc_ref[slot, rows]
            for r in range(1, rows - 1):
                y = jnp.maximum(acc_ref[slot, r + 1] + bias_ref[...], 0.0)
                hidden_ref[q, r * ch : (r + 1) * ch, :] = y.astype(BF16)
            for n in range(0, width, LANES):
                lanes = slice(n, n + LANES)
                y = jnp.dot(reg_ref[...], hidden_ref[q, :, lanes], preferred_element_type=F32)
                for a in range(3):
                    for c in range(3):
                        at = (a * 3 + c) * rows
                        sums_ref[c, first + q + 1 - a, :, lanes] += y[at : at + rows]

    @pl.when(s == last)
    def _():
        def finish(d, carry):
            cost_ref[d] = shifted(sums_ref[0, d], 1) + sums_ref[1, d] + shifted(sums_ref[2, d], -1)
            return carry

        lax.fori_loop(0, planes, finish, 0)


def inner(volume, weights, bias, reg):
    ch, planes, rows, width = volume.shape
    blocks = planes // 2
    whole = lambda x: pl.BlockSpec(x.shape, lambda s: (0,) * x.ndim)
    cost = jax.ShapeDtypeStruct((planes, rows, width), F32)
    pre = jax.ShapeDtypeStruct((planes - 2, 2, ch, width), F32)
    work = 2 * 27 * ch * ch * planes * rows * width
    return pl.pallas_call(
        inner_kernel,
        name="inner",
        grid=(blocks + 1,),
        out_shape=(cost, pre),
        in_specs=[
            pl.BlockSpec((ch, 2, rows, width), lambda s: (0, jnp.minimum(s, blocks - 1), 0, 0)),
            whole(weights), whole(bias), whole(reg),
        ],
        out_specs=(
            pl.BlockSpec(cost.shape, lambda s: (0, 0, 0)),
            pl.BlockSpec((2, 2, ch, width), lambda s: (jnp.maximum(s - 2, 0), 0, 0, 0)),
        ),
        scratch_shapes=[
            pltpu.VMEM((4, rows, 3 * ch, width), BF16),
            pltpu.VMEM((4, rows + 2, ch, width), F32),
            pltpu.VMEM((2, rows * ch, width), BF16),
            pltpu.VMEM((3, planes, rows, width), F32),
        ],
        compiler_params=ROOM,
        cost_estimate=pl.CostEstimate(
            flops=2 * work, bytes_accessed=volume.size * 2, transcendentals=0
        ),
    )(volume, weights, bias, reg)


def sides_kernel(
    side_ref, near_ref, pre_ref, above_ref, below_ref, bias_ref, reg_ref, out_ref, send_ref,
    taps_ref, acc_ref, hidden_ref, sums_ref,
):
    planes, _, width = out_ref.shape
    ch = near_ref.shape[1]
    side = side_ref[0]
    w = jnp.where(side == 0, below_ref[...], above_ref[...])
    e = 1 - side
    acc_ref[...] = jnp.zeros_like(acc_ref)
    sums_ref[...] = jnp.zeros_like(sums_ref)
    for d in range(planes):
        put(taps_ref, d // 2, d % 2, 0, near_ref[d][None])
    for k in range(planes // 2):
        for n in range(0, width, LANES):
            lanes = slice(n, n + LANES)
            x = taps_ref[k, :, :, lanes].reshape(6 * ch, LANES)
            y = jnp.dot(w, x, preferred_element_type=F32)
            for q in range(4):
                acc_ref[2 * k + q, :, lanes] += y[q * ch : (q + 1) * ch]
    for k in range(planes // 2 - 1):
        for p in range(2):
            d = 2 * k + 1 + p
            for row in range(2):
                y = pre_ref[d - 1, row] + jnp.where(e == row, acc_ref[d + 1], 0.0)
                y = jnp.maximum(y + bias_ref[...], 0.0).astype(BF16)
                hidden_ref[k, (2 * p + row) * ch : (2 * p + row + 1) * ch, :] = y
        for n in range(0, width, LANES):
            lanes = slice(n, n + LANES)
            y = jnp.dot(reg_ref[...], hidden_ref[k, :, lanes], preferred_element_type=F32)
            for q in range(4):
                sums_ref[2 * k + q, :, lanes] += y[q * 24 : (q + 1) * 24]
    for d in range(planes):
        y = sums_ref[d]
        right, left = shifted(y, 1), shifted(y, -1)
        total = right[0:6] + y[6:12] + left[12:18]
        out_ref[d, 0:6] = total
        send_ref[d : d + 1] = jnp.where(side == 0, total[5:6], total[0:1])


def sides(side, near, pre, above, below, bias, reg):
    ch, width = near.shape[1:]
    planes = near.shape[0] - 4
    return pl.pallas_call(
        sides_kernel,
        name="sides",
        out_shape=(
            jax.ShapeDtypeStruct((planes, 8, width), F32),
            jax.ShapeDtypeStruct((planes, width), F32),
        ),
        in_specs=[SMEM] + [VMEM] * 6,
        out_specs=(VMEM, VMEM),
        scratch_shapes=[
            pltpu.VMEM((planes // 2, 2, 3 * ch, width), BF16),
            pltpu.VMEM((planes + 2, ch, width), F32),
            pltpu.VMEM((planes // 2 - 1, 4 * ch, width), BF16),
            pltpu.VMEM((planes, 24, width), F32),
        ],
        compiler_params=ROOM,
        cost_estimate=pl.CostEstimate(flops=1 << 31, bytes_accessed=1 << 22, transcendentals=0),
    )(side, near, pre, above, below, bias, reg)


def outer_kernel(
    side_ref, vol_ref, near_ref, lo_ref, hi_ref, weight_ref, bias_ref, reg_ref, out_ref,
    taps_ref, hidden_ref,
):
    s = pl.program_id(0)
    ch, _, rows, width = vol_ref.shape
    planes = near_ref.shape[0] - 4
    half = ch // 2
    above = side_ref[0] == 1

    def stage_rows(slot, near, far):
        zero = jnp.zeros_like(near)
        put(taps_ref, slot, 0, 0, jnp.where(above, far, zero)[None])
        put(taps_ref, slot, 1, 0, jnp.where(above, near, zero)[None])
        put(taps_ref, slot, rows + 2, 0, jnp.where(above, zero, near)[None])
        put(taps_ref, slot, rows + 3, 0, jnp.where(above, zero, far)[None])

    low = s == 0
    for p in range(2):
        slot = 1 + p - s
        stage_rows(slot, near_ref[s * (planes - 2) + p], near_ref[planes + 2 * s + p])
        for h in range(2):
            block = vol_ref[h * half : (h + 1) * half, p]
            put(taps_ref, slot, 2, h * half, jnp.swapaxes(block, 0, 1))
    pick = lambda r: jnp.where(low, lo_ref[r], hi_ref[r])
    stage_rows(2 * s, pick(rows), pick(rows + 1))
    for r in range(0, rows, 4):
        put(taps_ref, 2 * s, 2 + r, 0, pick(slice(r, r + 4)))

    for j in range(rows // 2 + 1):
        for n in range(0, width, LANES):
            lanes = slice(n, n + LANES)
            sums = {}
            at = 0
            for blocks, outs in SINGLE:
                pieces = [
                    taps_ref[dd, 2 * j + hh, c0 * ch : c1 * ch, lanes] for dd, hh, c0, c1 in blocks
                ]
                x = jnp.concatenate(pieces, axis=0)
                w = weight_ref[at : at + len(outs) * ch, : x.shape[0]]
                y = jnp.dot(w, x, preferred_element_type=F32)
                for k, ho in enumerate(outs):
                    part = y[k * ch : (k + 1) * ch]
                    sums[ho] = sums[ho] + part if ho in sums else part
                at += len(outs) * ch
            for ho, y in sums.items():
                y = jnp.maximum(y + bias_ref[:, lanes], 0.0)
                r = 2 * j + ho
                if r == 0:
                    y = jnp.where(above, y, 0.0)
                if r == rows + 1:
                    y = jnp.where(above, 0.0, y)
                hidden_ref[r * ch : (r + 1) * ch, lanes] = y.astype(BF16)
    y = jnp.dot(reg_ref[...], hidden_ref[...], preferred_element_type=F32)
    for a in range(3):
        r = [y[(a * 3 + c) * rows : (a * 3 + c + 1) * rows] for c in range(3)]
        out_ref[0, 2 - a] = shifted(r[0], 1) + r[1] + shifted(r[2], -1)


def outer(side, volume, near, lo, hi, weights, bias, reg):
    ch, planes, rows, width = volume.shape
    whole = lambda x: pl.BlockSpec(x.shape, lambda s: (0,) * x.ndim)
    out = jax.ShapeDtypeStruct((2, 3, rows, width), F32)
    work = 2 * 27 * ch * ch * 2 * rows * width
    return pl.pallas_call(
        outer_kernel,
        name="outer",
        grid=(2,),
        out_shape=out,
        in_specs=[
            SMEM,
            pl.BlockSpec((ch, 2, rows, width), lambda s: (0, s * (planes // 2 - 1), 0, 0)),
            whole(near), whole(lo), whole(hi), whole(weights), whole(bias), whole(reg),
        ],
        out_specs=pl.BlockSpec((1, 3, rows, width), lambda s: (s, 0, 0, 0)),
        scratch_shapes=[
            pltpu.VMEM((3, rows + 4, 3 * ch, width), BF16),
            pltpu.VMEM(((rows + 2) * ch, width), BF16),
        ],
        compiler_params=ROOM,
        cost_estimate=pl.CostEstimate(flops=2 * work, bytes_accessed=1 << 22, transcendentals=0),
    )(side, volume, near, lo, hi, weights, bias, reg)


def stats_kernel(
    first_ref, side_ref, cost_ref, sides_ref, row_ref, outer_ref, out_ref, score_ref
):
    planes, rows, width = cost_ref.shape
    row = lax.broadcasted_iota(jnp.int32, (rows, width), 0)
    mine = jnp.where(side_ref[0] == 1, 0, rows - 1)

    def cost_of(d):
        cost = cost_ref[d]
        for k, r in ((1, 0), (2, 1), (3, rows - 2), (4, rows - 1)):
            cost = cost + jnp.where(row == r, sides_ref[d, k : k + 1], 0.0)
        return cost + jnp.where(row == mine, row_ref[d : d + 1], 0.0)

    extra = {0: outer_ref[0, 1], 1: outer_ref[0, 2]}
    for d, x in ((planes - 2, outer_ref[1, 0]), (planes - 1, outer_ref[1, 1])):
        extra[d] = x if d not in extra else extra[d] + x
    peak = None
    for d in range(1, planes - 1):
        cost = cost_of(d)
        if d in extra:
            cost = cost + extra[d]
        score = -cost
        score_ref[d] = score
        peak = score if peak is None else jnp.maximum(peak, score)
    total = jnp.zeros((rows, width), F32)
    moment = jnp.zeros((rows, width), F32)
    first = first_ref[0].astype(F32)
    for d in range(1, planes - 1):
        expo = jnp.exp(score_ref[d] - peak)
        total = total + expo
        moment = moment + (first + float(d)) * expo
    values = (
        peak, total, moment, cost_of(0) + extra[0], cost_of(planes - 1) + extra[planes - 1],
        outer_ref[0, 0], outer_ref[1, 2], jnp.zeros((rows, width), F32),
    )
    for k, value in enumerate(values):
        for t in range(rows // 8):
            for u in range(width // 128):
                tile = value[t * 8 : (t + 1) * 8, u * 128 : (u + 1) * 128]
                out_ref[t * (width // 128) + u, k] = tile


def stats(first, side, cost, sides_cost, row, outer_cost):
    planes, rows, width = cost.shape
    return pl.pallas_call(
        stats_kernel,
        name="stats",
        out_shape=jax.ShapeDtypeStruct((rows * width // 1024, 8, 8, 128), F32),
        in_specs=[SMEM, SMEM] + [VMEM] * 4,
        out_specs=VMEM,
        scratch_shapes=[pltpu.VMEM((planes, rows, width), F32)],
        compiler_params=ROOM,
    )(first, side, cost, sides_cost, row, outer_cost)


def join_kernel(planes, in_ref, out_ref):
    count = in_ref.shape[0]
    scores = []
    peak = None
    for j in range(count):
        low, high = in_ref[j, 3], in_ref[j, 4]
        if j > 0:
            low = low + in_ref[j - 1, 6]
        if j < count - 1:
            high = high + in_ref[j + 1, 5]
        scores.append((-low, -high))
        here = jnp.maximum(in_ref[j, 0], jnp.maximum(-low, -high))
        peak = here if peak is None else jnp.maximum(peak, here)
    total = jnp.zeros_like(peak)
    moment = jnp.zeros_like(peak)
    for j in range(count):
        scale = jnp.exp(in_ref[j, 0] - peak)
        low, high = (jnp.exp(score - peak) for score in scores[j])
        total = total + in_ref[j, 1] * scale + low + high
        ends = float(j * planes) * low + float((j + 1) * planes - 1) * high
        moment = moment + in_ref[j, 2] * scale + ends
    result = moment / total
    for j in range(count):
        out_ref[j] = result


def join(pieces, planes):
    count, _, rows, width = pieces.shape
    return pl.pallas_call(
        functools.partial(join_kernel, planes),
        name="join",
        out_shape=jax.ShapeDtypeStruct((count, rows, width), F32),
        in_specs=[VMEM],
        out_specs=VMEM,
        compiler_params=ROOM,
    )(pieces)


def joined(values, planes, rows, width):
    count = lax.axis_size("disp")
    tiles = values.shape[0]
    if count > tiles:
        parts = count // tiles
        values = values.reshape(tiles, 8, parts, 8 // parts, 128)
        values = jnp.swapaxes(values, 1, 2).reshape(count, 8, 8 // parts, 128)
    elif count < tiles:
        parts = tiles // count
        values = values.reshape(count, parts, 8, 8, 128)
        values = jnp.swapaxes(values, 1, 2).reshape(count, 8, parts * 8, 128)
    pieces = lax.all_to_all(values, "disp", 0, 0)
    result = lax.all_to_all(join(pieces, planes), "disp", 0, 0)
    result = result.reshape(rows // 8, width // 128, 8, 128)
    return jnp.swapaxes(result, 1, 2).reshape(rows, width)


def exchange(x, axis):
    return lax.ppermute(x, axis, [(0, 1), (1, 0)] if lax.axis_size(axis) == 2 else [])


def up(x, axis):
    count = lax.axis_size(axis)
    return lax.ppermute(x, axis, [(i, i + 1) for i in range(count - 1)])


def down(x, axis):
    count = lax.axis_size(axis)
    return lax.ppermute(x, axis, [(i + 1, i) for i in range(count - 1)])


def body(volume, conv_weight, conv_bias, reg_weight):
    ch, planes, rows, width = volume.shape
    bias = jnp.broadcast_to(conv_bias[:, None], (ch, width))
    side = lax.axis_index("rows").astype(jnp.int32).reshape(1)
    first = (lax.axis_index("disp") * planes).astype(jnp.int32).reshape(1)

    near, first_plane, last_plane = edges(side, volume)
    near = exchange(near, "rows")
    spread, above, below, single = packed(conv_weight)
    reg_inner = regression_rows(reg_weight, rows, rows, 0)
    reg_outer = regression_rows(reg_weight, rows, rows + 2, -1)
    reg_edges = regression_edges(reg_weight, rows)
    ends = [near[planes - 1], near[planes + 3]], [near[0], near[planes]]
    lo = up(jnp.concatenate([last_plane, jnp.stack(ends[0])]), "disp")
    hi = down(jnp.concatenate([first_plane, jnp.stack(ends[1])]), "disp")

    cost, pre = inner(volume, spread, bias, reg_inner)
    sides_cost, send = sides(side, near, pre, above, below, bias, reg_edges)
    row = exchange(send, "rows")
    outer_cost = outer(side, volume, near, lo, hi, single, bias, reg_outer)
    values = stats(first, side, cost, sides_cost, row, outer_cost)
    return joined(values, planes, rows, width)


def solution(mesh):
    in_specs = (P(None, "disp", ("tiles", "rows"), None), P(), P(), P())
    out_specs = P(("tiles", "rows"), None)
    return jax.shard_map(body, mesh=mesh, in_specs=in_specs, out_specs=out_specs, check_vma=False)
```

```python
import functools

import jax
import jax.numpy as jnp
import numpy as np
from jax import lax
from jax.experimental import pallas as pl
from jax.experimental.pallas import tpu as pltpu
from jax.sharding import PartitionSpec as P

BF16 = jnp.bfloat16
F32 = jnp.float32
LANES = 256
VMEM = pl.BlockSpec(memory_space=pltpu.VMEM)
SMEM = pl.BlockSpec(memory_space=pltpu.SMEM)
ROOM = pltpu.CompilerParams(vmem_limit_bytes=48 << 20)

SINGLE = (
    (((0, 0, 0, 3), (1, 0, 0, 3), (2, 0, 0, 2)), (0,)),
    (((0, 3, 0, 3), (1, 3, 0, 3), (2, 3, 0, 2)), (1,)),
    (((0, 1, 0, 3), (0, 2, 0, 3), (1, 1, 0, 2)), (0, 1)),
    (((1, 1, 2, 3), (1, 2, 0, 3), (2, 1, 0, 3), (2, 2, 0, 1)), (0, 1)),
    (((2, 2, 1, 3), (2, 0, 2, 3), (2, 3, 2, 3)), (0, 1)),
)


def tap(a, b, c):
    return 9 * a + 3 * b + c if 0 <= a < 3 and 0 <= b < 3 else None


def single_table():
    table = []
    for blocks, outs in SINGLE:
        for ho in outs:
            row = [tap(dd, hh - ho, c) for dd, hh, c0, c1 in blocks for c in range(c0, c1)]
            table.append(row + [None] * (8 - len(row)))
    return table


def spread_table():
    return [
        [tap(2 - do, hi - ho + 2, c) for hi in range(2) for c in range(3)]
        for ho in range(4) for do in range(3)
    ]


def halo_table(b):
    return [[tap(p - q + 2, b, c) for p in range(2) for c in range(3)] for q in range(4)]


def pack_kernel(tables, rows, conv_ref, bias_ref, reg_ref, *refs):
    ch = conv_ref.shape[1]
    weight_refs = refs[: len(tables)]
    wide_ref, inner_ref, outer_ref, edges_ref, turn_ref, line_ref, sparse_ref = refs[len(tables) :]
    for table, out_ref in zip(tables, weight_refs):
        for m, row in enumerate(table):
            for k, t in enumerate(row):
                block = jnp.zeros((ch, ch), BF16) if t is None else conv_ref[t]
                out_ref[m * ch : (m + 1) * ch, k * ch : (k + 1) * ch] = block
    wide_ref[...] = jnp.broadcast_to(bias_ref[...], wide_ref.shape)
    size = turn_ref.shape[0]
    r = lax.broadcasted_iota(jnp.int32, (size, size), 0)
    k = lax.broadcasted_iota(jnp.int32, (size, size), 1)
    half = size // rows
    hit = k == (r % half) * rows + r // half
    turn_ref[...] = jnp.where(hit, 1.0, 0.0).astype(BF16)

    reg = reg_ref[...].astype(F32)
    line_ref[...] = jnp.zeros_like(line_ref)
    sparse_ref[...] = jnp.zeros_like(sparse_ref)
    for a in range(3):
        for b in range(3):
            for c in range(3):
                t = tap(a, b, c)
                one = reg[t : t + 1]
                line_ref[a * 3 + c : a * 3 + c + 1, b * ch : (b + 1) * ch] = one
                for p in range(2):
                    q = p + 2 - a
                    for e in range(2):
                        at = q * 24 + c * 6 + (2 - b) + 3 * e
                        col = (2 * p + e) * ch
                        sparse_ref[at : at + 1, col : col + ch] = one
    edges_ref[...] = sparse_ref[...].astype(BF16)
    width = line_ref.shape[1]
    row = lax.broadcasted_iota(jnp.int32, (rows, width), 0)
    for k in range(9):
        x = jnp.broadcast_to(line_ref[k : k + 1], (rows, width))
        step = 1
        while step < rows:
            x = jnp.where((row & step) != 0, pltpu.roll(x, step * ch, 1), x)
            step *= 2
        at = slice(k * rows, (k + 1) * rows)
        outer_ref[at] = x[:, : (rows + 2) * ch].astype(BF16)
        inner_ref[at] = pltpu.roll(x, width - ch, 1)[:, : rows * ch].astype(BF16)


def packed(conv_weight, conv_bias, reg_weight, rows, width):
    ch = conv_weight.shape[1]
    tables = [spread_table(), halo_table(0), halo_table(2), single_table()]
    shapes = [((len(t) * ch, len(t[0]) * ch), BF16) for t in tables]
    shapes += [
        ((ch, width), F32), ((9 * rows, rows * ch), BF16), ((9 * rows, (rows + 2) * ch), BF16),
        ((96, 4 * ch), BF16), ((rows * ch // 2, rows * ch // 2), BF16),
    ]
    outs = [jax.ShapeDtypeStruct(*x) for x in shapes]
    line = -(-(rows + 3) * ch // 128) * 128
    return pl.pallas_call(
        functools.partial(pack_kernel, tables, rows),
        name="pack",
        out_shape=outs,
        in_specs=[VMEM] * 3,
        out_specs=[VMEM] * len(outs),
        scratch_shapes=[pltpu.VMEM((16, line), F32), pltpu.VMEM((96, 4 * ch), F32)],
        compiler_params=ROOM,
    )(conv_weight, conv_bias[:, None], reg_weight)


def shifted(x, by):
    width = x.shape[-1]
    moved = pltpu.roll(x, by % width, x.ndim - 1)
    lane = lax.broadcasted_iota(jnp.int32, x.shape[:-1] + (128,), x.ndim - 1)
    zero = jnp.zeros(x.shape[:-1] + (128,), x.dtype)
    if by == 1:
        edge = jnp.where(lane == 0, zero, moved[..., :128])
        return jnp.concatenate([edge, moved[..., 128:]], axis=-1)
    edge = jnp.where(lane == 127, zero, moved[..., width - 128 :])
    return jnp.concatenate([moved[..., : width - 128], edge], axis=-1)


def put(taps_ref, slot, row, at, x):
    count, size, width = x.shape
    ch = taps_ref.shape[2] // 3
    flat = x.reshape(count * size, width)
    for c, y in ((0, shifted(flat, 1)), (1, flat), (2, shifted(flat, -1))):
        taps_ref[slot, pl.ds(row, count), pl.ds(c * ch + at, size), :] = y.reshape(x.shape)


def turn(taps_ref, slot, row, at, block, turn_ref):
    size, rows, width = block.shape
    ch = taps_ref.shape[2] // 3
    y = jnp.dot(turn_ref[...], block.reshape(size * rows, width), preferred_element_type=F32)
    taps_ref[slot, pl.ds(row, rows), ch + at : ch + at + size, :] = (
        y.astype(BF16).reshape(rows, size, width)
    )


def spread(taps_ref, slot, row, count):
    width = taps_ref.shape[3]
    ch = taps_ref.shape[2] // 3
    x = taps_ref[slot, pl.ds(row, count), ch : 2 * ch, :].reshape(count * ch, width)
    taps_ref[slot, pl.ds(row, count), :ch, :] = shifted(x, 1).reshape(count, ch, width)
    taps_ref[slot, pl.ds(row, count), 2 * ch :, :] = shifted(x, -1).reshape(count, ch, width)


def edges_kernel(side_ref, vol_ref, near_ref, first_ref, last_ref, pick_ref):
    s = pl.program_id(0)
    steps = pl.num_programs(0)
    ch, _, rows, width = vol_ref.shape
    planes = 2 * steps

    @pl.when(s == 0)
    def _():
        r = lax.broadcasted_iota(jnp.int32, pick_ref.shape, 0)
        k = lax.broadcasted_iota(jnp.int32, pick_ref.shape, 1)
        far = jnp.where(r >= ch, 1, 0)
        row = jnp.where(side_ref[0] == 0, rows - 1 - far, far)
        pick_ref[...] = jnp.where(k == (r - ch * far) * rows + row, 1.0, 0.0).astype(BF16)

    def rows_of(p, part):
        x = vol_ref[:, p].reshape(ch * rows, width)
        w = pick_ref[part * ch : (part + 1) * ch]
        return jnp.dot(w, x, preferred_element_type=F32).astype(BF16)

    for p in range(2):
        near_ref[2 * s + p] = rows_of(p, 0)

    @pl.when((s == 0) | (s == steps - 1))
    def _():
        for p in range(2):
            near_ref[planes + p + jnp.where(s == 0, 0, 2)] = rows_of(p, 1)

    @pl.when(s == 0)
    def _():
        first_ref[0] = near_ref[0]
        first_ref[1] = near_ref[planes]

    @pl.when(s == steps - 1)
    def _():
        last_ref[0] = near_ref[planes - 1]
        last_ref[1] = near_ref[planes + 3]


def edges(side, volume):
    ch, planes, rows, width = volume.shape
    near = jax.ShapeDtypeStruct((planes + 4, ch, width), BF16)
    corner = jax.ShapeDtypeStruct((2, ch, width), BF16)
    zero = lambda s: (0, 0, 0)
    return pl.pallas_call(
        edges_kernel,
        name="edges",
        grid=(planes // 2,),
        out_shape=(near, corner, corner),
        in_specs=[SMEM, pl.BlockSpec((ch, 2, rows, width), lambda s: (0, s, 0, 0))],
        out_specs=[pl.BlockSpec(x.shape, zero) for x in (near, corner, corner)],
        scratch_shapes=[pltpu.VMEM((2 * ch, ch * rows), BF16)],
        compiler_params=ROOM,
        cost_estimate=pl.CostEstimate(
            flops=1 << 30, bytes_accessed=volume.size * 2, transcendentals=0
        ),
    )(side, volume)


def inner_kernel(
    vol_ref, weight_ref, bias_ref, reg_ref, turn_ref, cost_ref, pre_ref,
    taps_ref, acc_ref, hidden_ref, sums_ref,
):
    s = pl.program_id(0)
    last = pl.num_programs(0) - 1
    ch, _, rows, width = vol_ref.shape
    planes = cost_ref.shape[0]
    half = ch // 2
    new = (s % 2) * 2
    old = ((s + 1) % 2) * 2

    def stage(part):
        p, h = part // 4, part % 4
        if h < 2:
            block = vol_ref[h * half : (h + 1) * half, p]
            turn(taps_ref, new + p, 0, h * half, block, turn_ref)
        else:
            spread(taps_ref, new + p, (h - 2) * (rows // 2), rows // 2)

    @pl.when(s == 0)
    def _():
        for part in range(8):
            stage(part)
        sums_ref[...] = jnp.zeros_like(sums_ref)
        hidden_ref[...] = jnp.zeros_like(hidden_ref)

    @pl.when(s >= 1)
    def _():
        base = 2 * (s - 1) + 3
        tiles = rows // 2
        for p in range(2):
            slots = [(base + p + do) % 4 for do in range(3)]
            for j in range(tiles):
                ho0 = 1 if j == 0 else 0
                ho1 = 3 if j == tiles - 1 else 4
                w = weight_ref[ho0 * 3 * ch : ho1 * 3 * ch]
                for n in range(0, width, LANES):
                    lanes = slice(n, n + LANES)
                    x = taps_ref[old + p, 2 * j : 2 * j + 2, :, lanes].reshape(6 * ch, LANES)
                    y = jnp.dot(w, x, preferred_element_type=F32)
                    for ho in range(ho0, ho1):
                        for do in range(3):
                            at = ((ho - ho0) * 3 + do) * ch
                            part = y[at : at + ch]
                            fresh = do == 2 and (ho >= 2 or j == 0)
                            if not fresh:
                                part = part + acc_ref[slots[do], 2 * j + ho, :, lanes]
                            acc_ref[slots[do], 2 * j + ho, :, lanes] = part
                if (j + 1) * 4 // tiles > j * 4 // tiles:
                    stage(4 * p + j * 4 // tiles)

    @pl.when(s >= 2)
    def _():
        first = 2 * (s - 1) - 1
        for q in range(2):
            slot = (first + q) % 4
            pre_ref[q, 0] = acc_ref[slot, 1]
            pre_ref[q, 1] = acc_ref[slot, rows]
            for r in range(1, rows - 1):
                y = jnp.maximum(acc_ref[slot, r + 1] + bias_ref[...], 0.0)
                hidden_ref[q, r * ch : (r + 1) * ch, :] = y.astype(BF16)
            for n in range(0, width, LANES):
                lanes = slice(n, n + LANES)
                y = jnp.dot(reg_ref[...], hidden_ref[q, :, lanes], preferred_element_type=F32)
                for a in range(3):
                    for c in range(3):
                        at = (a * 3 + c) * rows
                        sums_ref[c, first + q + 1 - a, :, lanes] += y[at : at + rows]

    @pl.when(s == last)
    def _():
        def finish(d, carry):
            cost_ref[d] = shifted(sums_ref[0, d], 1) + sums_ref[1, d] + shifted(sums_ref[2, d], -1)
            return carry

        lax.fori_loop(0, planes, finish, 0)


def inner(volume, weights, bias, reg, turning):
    ch, planes, rows, width = volume.shape
    blocks = planes // 2
    whole = lambda x: pl.BlockSpec(x.shape, lambda s: (0,) * x.ndim)
    cost = jax.ShapeDtypeStruct((planes, rows, width), F32)
    pre = jax.ShapeDtypeStruct((planes - 2, 2, ch, width), F32)
    work = 2 * 27 * ch * ch * planes * rows * width
    return pl.pallas_call(
        inner_kernel,
        name="inner",
        grid=(blocks + 1,),
        out_shape=(cost, pre),
        in_specs=[
            pl.BlockSpec((ch, 2, rows, width), lambda s: (0, jnp.minimum(s, blocks - 1), 0, 0)),
            whole(weights), whole(bias), whole(reg), whole(turning),
        ],
        out_specs=(
            pl.BlockSpec(cost.shape, lambda s: (0, 0, 0)),
            pl.BlockSpec((2, 2, ch, width), lambda s: (jnp.maximum(s - 2, 0), 0, 0, 0)),
        ),
        scratch_shapes=[
            pltpu.VMEM((4, rows, 3 * ch, width), BF16),
            pltpu.VMEM((4, rows + 2, ch, width), F32),
            pltpu.VMEM((2, rows * ch, width), BF16),
            pltpu.VMEM((3, planes, rows, width), F32),
        ],
        compiler_params=ROOM,
        cost_estimate=pl.CostEstimate(
            flops=2 * work, bytes_accessed=volume.size * 2, transcendentals=0
        ),
    )(volume, weights, bias, reg, turning)


def sides_kernel(
    side_ref, near_ref, pre_ref, above_ref, below_ref, bias_ref, reg_ref, out_ref, send_ref,
    taps_ref, acc_ref, hidden_ref, sums_ref,
):
    planes, _, width = out_ref.shape
    ch = near_ref.shape[1]
    side = side_ref[0]
    w = jnp.where(side == 0, below_ref[...], above_ref[...])
    e = 1 - side
    acc_ref[...] = jnp.zeros_like(acc_ref)
    sums_ref[...] = jnp.zeros_like(sums_ref)
    for d in range(planes):
        put(taps_ref, d // 2, d % 2, 0, near_ref[d][None])
    for k in range(planes // 2):
        for n in range(0, width, LANES):
            lanes = slice(n, n + LANES)
            x = taps_ref[k, :, :, lanes].reshape(6 * ch, LANES)
            y = jnp.dot(w, x, preferred_element_type=F32)
            for q in range(4):
                acc_ref[2 * k + q, :, lanes] += y[q * ch : (q + 1) * ch]
    for k in range(planes // 2 - 1):
        for p in range(2):
            d = 2 * k + 1 + p
            for row in range(2):
                y = pre_ref[d - 1, row] + jnp.where(e == row, acc_ref[d + 1], 0.0)
                y = jnp.maximum(y + bias_ref[...], 0.0).astype(BF16)
                hidden_ref[k, (2 * p + row) * ch : (2 * p + row + 1) * ch, :] = y
        for n in range(0, width, LANES):
            lanes = slice(n, n + LANES)
            y = jnp.dot(reg_ref[...], hidden_ref[k, :, lanes], preferred_element_type=F32)
            for q in range(4):
                sums_ref[2 * k + q, :, lanes] += y[q * 24 : (q + 1) * 24]
    for d in range(planes):
        y = sums_ref[d]
        right, left = shifted(y, 1), shifted(y, -1)
        total = right[0:6] + y[6:12] + left[12:18]
        out_ref[d, 0:6] = total
        send_ref[d : d + 1] = jnp.where(side == 0, total[5:6], total[0:1])


def sides(side, near, pre, above, below, bias, reg):
    ch, width = near.shape[1:]
    planes = near.shape[0] - 4
    return pl.pallas_call(
        sides_kernel,
        name="sides",
        out_shape=(
            jax.ShapeDtypeStruct((planes, 8, width), F32),
            jax.ShapeDtypeStruct((planes, width), F32),
        ),
        in_specs=[SMEM] + [VMEM] * 6,
        out_specs=(VMEM, VMEM),
        scratch_shapes=[
            pltpu.VMEM((planes // 2, 2, 3 * ch, width), BF16),
            pltpu.VMEM((planes + 2, ch, width), F32),
            pltpu.VMEM((planes // 2 - 1, 4 * ch, width), BF16),
            pltpu.VMEM((planes, 24, width), F32),
        ],
        compiler_params=ROOM,
        cost_estimate=pl.CostEstimate(flops=1 << 31, bytes_accessed=1 << 22, transcendentals=0),
    )(side, near, pre, above, below, bias, reg)


def outer_kernel(
    side_ref, vol_ref, near_ref, lo_ref, hi_ref, lo_rows_ref, hi_rows_ref, weight_ref, bias_ref,
    reg_ref, turn_ref, out_ref, taps_ref, hidden_ref,
):
    s = pl.program_id(0)
    ch, _, rows, width = vol_ref.shape
    planes = near_ref.shape[0] - 4
    half = ch // 2
    above = side_ref[0] == 1

    def stage_rows(slot, near, far):
        zero = jnp.zeros_like(near)
        put(taps_ref, slot, 0, 0, jnp.where(above, far, zero)[None])
        put(taps_ref, slot, 1, 0, jnp.where(above, near, zero)[None])
        put(taps_ref, slot, rows + 2, 0, jnp.where(above, zero, near)[None])
        put(taps_ref, slot, rows + 3, 0, jnp.where(above, zero, far)[None])

    low = s == 0
    for p in range(2):
        stage_rows(1 + p - s, near_ref[s * (planes - 2) + p], near_ref[planes + 2 * s + p])
    corner = jnp.where(low, lo_rows_ref[...], hi_rows_ref[...])
    stage_rows(2 * s, corner[0], corner[1])
    for h in range(2):
        part = slice(h * half, (h + 1) * half)
        for p in range(2):
            turn(taps_ref, 1 + p - s, 2, h * half, vol_ref[part, p], turn_ref)
        far_block = jnp.where(low, lo_ref[part], hi_ref[part])
        turn(taps_ref, 2 * s, 2, h * half, far_block, turn_ref)
    for slot in range(3):
        for r in range(0, rows, rows // 2):
            spread(taps_ref, slot, 2 + r, rows // 2)

    for j in range(rows // 2 + 1):
        for n in range(0, width, LANES):
            lanes = slice(n, n + LANES)
            sums = {}
            at = 0
            for blocks, outs in SINGLE:
                pieces = [
                    taps_ref[dd, 2 * j + hh, c0 * ch : c1 * ch, lanes] for dd, hh, c0, c1 in blocks
                ]
                x = jnp.concatenate(pieces, axis=0)
                w = weight_ref[at : at + len(outs) * ch, : x.shape[0]]
                y = jnp.dot(w, x, preferred_element_type=F32)
                for k, ho in enumerate(outs):
                    part = y[k * ch : (k + 1) * ch]
                    sums[ho] = sums[ho] + part if ho in sums else part
                at += len(outs) * ch
            for ho, y in sums.items():
                y = jnp.maximum(y + bias_ref[:, lanes], 0.0)
                r = 2 * j + ho
                if r == 0:
                    y = jnp.where(above, y, 0.0)
                if r == rows + 1:
                    y = jnp.where(above, 0.0, y)
                hidden_ref[r * ch : (r + 1) * ch, lanes] = y.astype(BF16)
    y = jnp.dot(reg_ref[...], hidden_ref[...], preferred_element_type=F32)
    for a in range(3):
        r = [y[(a * 3 + c) * rows : (a * 3 + c + 1) * rows] for c in range(3)]
        out_ref[0, 2 - a] = shifted(r[0], 1) + r[1] + shifted(r[2], -1)


def outer(side, volume, near, halos, weights, bias, reg, turning):
    ch, planes, rows, width = volume.shape
    whole = lambda x: pl.BlockSpec(x.shape, lambda s: (0,) * x.ndim)
    out = jax.ShapeDtypeStruct((2, 3, rows, width), F32)
    work = 2 * 27 * ch * ch * 2 * rows * width
    return pl.pallas_call(
        outer_kernel,
        name="outer",
        grid=(2,),
        out_shape=out,
        in_specs=[
            SMEM,
            pl.BlockSpec((ch, 2, rows, width), lambda s: (0, s * (planes // 2 - 1), 0, 0)),
            whole(near), *map(whole, halos), whole(weights), whole(bias), whole(reg),
            whole(turning),
        ],
        out_specs=pl.BlockSpec((1, 3, rows, width), lambda s: (s, 0, 0, 0)),
        scratch_shapes=[
            pltpu.VMEM((3, rows + 4, 3 * ch, width), BF16),
            pltpu.VMEM(((rows + 2) * ch, width), BF16),
        ],
        compiler_params=ROOM,
        cost_estimate=pl.CostEstimate(flops=2 * work, bytes_accessed=1 << 22, transcendentals=0),
    )(side, volume, near, *halos, weights, bias, reg, turning)


def stats_kernel(
    first_ref, side_ref, cost_ref, sides_ref, row_ref, outer_ref, out_ref, score_ref
):
    planes, rows, width = cost_ref.shape
    row = lax.broadcasted_iota(jnp.int32, (rows, width), 0)
    mine = jnp.where(side_ref[0] == 1, 0, rows - 1)

    def cost_of(d):
        cost = cost_ref[d]
        for k, r in ((1, 0), (2, 1), (3, rows - 2), (4, rows - 1)):
            cost = cost + jnp.where(row == r, sides_ref[d, k : k + 1], 0.0)
        return cost + jnp.where(row == mine, row_ref[d : d + 1], 0.0)

    extra = {0: outer_ref[0, 1], 1: outer_ref[0, 2]}
    for d, x in ((planes - 2, outer_ref[1, 0]), (planes - 1, outer_ref[1, 1])):
        extra[d] = x if d not in extra else extra[d] + x
    peak = None
    for d in range(1, planes - 1):
        cost = cost_of(d)
        if d in extra:
            cost = cost + extra[d]
        score = -cost
        score_ref[d] = score
        peak = score if peak is None else jnp.maximum(peak, score)
    total = jnp.zeros((rows, width), F32)
    moment = jnp.zeros((rows, width), F32)
    first = first_ref[0].astype(F32)
    for d in range(1, planes - 1):
        expo = jnp.exp(score_ref[d] - peak)
        total = total + expo
        moment = moment + (first + float(d)) * expo
    values = (
        peak, total, moment, cost_of(0) + extra[0], cost_of(planes - 1) + extra[planes - 1],
        outer_ref[0, 0], outer_ref[1, 2], jnp.zeros((rows, width), F32),
    )
    for k, value in enumerate(values):
        for t in range(rows // 8):
            for u in range(width // 128):
                tile = value[t * 8 : (t + 1) * 8, u * 128 : (u + 1) * 128]
                out_ref[t * (width // 128) + u, k] = tile


def stats(first, side, cost, sides_cost, row, outer_cost):
    planes, rows, width = cost.shape
    return pl.pallas_call(
        stats_kernel,
        name="stats",
        out_shape=jax.ShapeDtypeStruct((rows * width // 1024, 8, 8, 128), F32),
        in_specs=[SMEM, SMEM] + [VMEM] * 4,
        out_specs=VMEM,
        scratch_shapes=[pltpu.VMEM((planes, rows, width), F32)],
        compiler_params=ROOM,
    )(first, side, cost, sides_cost, row, outer_cost)


def join_kernel(planes, in_ref, out_ref):
    count = in_ref.shape[0]
    scores = []
    peak = None
    for j in range(count):
        low, high = in_ref[j, 3], in_ref[j, 4]
        if j > 0:
            low = low + in_ref[j - 1, 6]
        if j < count - 1:
            high = high + in_ref[j + 1, 5]
        scores.append((-low, -high))
        here = jnp.maximum(in_ref[j, 0], jnp.maximum(-low, -high))
        peak = here if peak is None else jnp.maximum(peak, here)
    total = jnp.zeros_like(peak)
    moment = jnp.zeros_like(peak)
    for j in range(count):
        scale = jnp.exp(in_ref[j, 0] - peak)
        low, high = (jnp.exp(score - peak) for score in scores[j])
        total = total + in_ref[j, 1] * scale + low + high
        ends = float(j * planes) * low + float((j + 1) * planes - 1) * high
        moment = moment + in_ref[j, 2] * scale + ends
    result = moment / total
    for j in range(count):
        out_ref[j] = result


def join(pieces, planes):
    count, _, rows, width = pieces.shape
    return pl.pallas_call(
        functools.partial(join_kernel, planes),
        name="join",
        out_shape=jax.ShapeDtypeStruct((count, rows, width), F32),
        in_specs=[VMEM],
        out_specs=VMEM,
        compiler_params=ROOM,
    )(pieces)


def joined(values, planes, rows, width):
    count = lax.axis_size("disp")
    tiles = values.shape[0]
    if count > tiles:
        parts = count // tiles
        values = values.reshape(tiles, 8, parts, 8 // parts, 128)
        values = jnp.swapaxes(values, 1, 2).reshape(count, 8, 8 // parts, 128)
    elif count < tiles:
        parts = tiles // count
        values = values.reshape(count, parts, 8, 8, 128)
        values = jnp.swapaxes(values, 1, 2).reshape(count, 8, parts * 8, 128)
    pieces = lax.all_to_all(values, "disp", 0, 0)
    result = lax.all_to_all(join(pieces, planes), "disp", 0, 0)
    result = result.reshape(rows // 8, width // 128, 8, 128)
    return jnp.swapaxes(result, 1, 2).reshape(rows, width)


def exchange(x, axis):
    return lax.ppermute(x, axis, [(0, 1), (1, 0)] if lax.axis_size(axis) == 2 else [])


def up(x, axis):
    count = lax.axis_size(axis)
    return lax.ppermute(x, axis, [(i, i + 1) for i in range(count - 1)])


def down(x, axis):
    count = lax.axis_size(axis)
    return lax.ppermute(x, axis, [(i + 1, i) for i in range(count - 1)])


def across(x, step):
    count = lax.axis_size("disp")
    sides = lax.axis_size("rows")
    pairs = [
        (i * sides + r, (i + step) * sides + 1 - r)
        for i in range(count) for r in range(sides)
        if 0 <= i + step < count and sides == 2
    ]
    return lax.ppermute(x, ("disp", "rows"), pairs)


def body(volume, conv_weight, conv_bias, reg_weight):
    ch, planes, rows, width = volume.shape
    side = lax.axis_index("rows").astype(jnp.int32).reshape(1)
    first = (lax.axis_index("disp") * planes).astype(jnp.int32).reshape(1)

    ends = volume[:, planes - 1], volume[:, 0]
    volume, ends = lax.optimization_barrier((volume, ends))
    lo = up(ends[0], "disp")
    hi = down(ends[1], "disp")
    near, first_rows, last_rows = edges(side, volume)
    near = exchange(near, "rows")
    lo_rows = across(last_rows, 1)
    hi_rows = across(first_rows, -1)
    spread_w, above, below, single, bias, reg_inner, reg_outer, reg_edges, turning = packed(
        conv_weight, conv_bias, reg_weight, rows, width
    )

    cost, pre = inner(volume, spread_w, bias, reg_inner, turning)
    sides_cost, send = sides(side, near, pre, above, below, bias, reg_edges)
    row = exchange(send, "rows")
    halos = (lo, hi, lo_rows, hi_rows)
    outer_cost = outer(side, volume, near, halos, single, bias, reg_outer, turning)
    values = stats(first, side, cost, sides_cost, row, outer_cost)
    return joined(values, planes, rows, width)


def solution(mesh):
    in_specs = (P(None, "disp", ("tiles", "rows"), None), P(), P(), P())
    out_specs = P(("tiles", "rows"), None)
    return jax.shard_map(body, mesh=mesh, in_specs=in_specs, out_specs=out_specs, check_vma=False)
```

```python
import functools

import jax
import jax.numpy as jnp
import numpy as np
from jax import lax
from jax.experimental import pallas as pl
from jax.experimental.pallas import tpu as pltpu
from jax.sharding import PartitionSpec as P

BF16 = jnp.bfloat16
F32 = jnp.float32
SMEM = pl.BlockSpec(memory_space=pltpu.SMEM)
ROOM = pltpu.CompilerParams(vmem_limit_bytes=32 << 20)


def whole(x):
    return pl.BlockSpec(x.shape, lambda s: (0,) * x.ndim)

SINGLE = (
    (((0, 0, 0, 3), (1, 0, 0, 3), (2, 0, 0, 2)), (0,)),
    (((0, 3, 0, 3), (1, 3, 0, 3), (2, 3, 0, 2)), (1,)),
    (((0, 1, 0, 3), (0, 2, 0, 3), (1, 1, 0, 2)), (0, 1)),
    (((1, 1, 2, 3), (1, 2, 0, 3), (2, 1, 0, 3), (2, 2, 0, 1)), (0, 1)),
    (((2, 2, 1, 3), (2, 0, 2, 3), (2, 3, 2, 3)), (0, 1)),
)


def tap(a, b, c):
    return 9 * a + 3 * b + c if 0 <= a < 3 and 0 <= b < 3 else None


def single_table():
    table = []
    for blocks, outs in SINGLE:
        for ho in outs:
            row = [tap(dd, hh - ho, c) for dd, hh, c0, c1 in blocks for c in range(c0, c1)]
            table.append(row + [None] * (8 - len(row)))
    return table


def spread_table():
    return [
        [tap(2 - do, hi - ho + 2, c) for hi in range(2) for c in range(3)]
        for ho in range(4) for do in range(3)
    ]


def halo_table(b):
    return [[tap(p - q + 2, b, c) for p in range(2) for c in range(3)] for q in range(4)]


def pick_rows(side, width, rows):
    ch = width // rows
    r = lax.broadcasted_iota(jnp.int32, (2 * ch, width), 0)
    k = lax.broadcasted_iota(jnp.int32, (2 * ch, width), 1)
    far = jnp.where(r >= ch, 1, 0)
    row = jnp.where(side == 0, rows - 1 - far, far)
    return jnp.where(k == (r - ch * far) * rows + row, 1.0, 0.0).astype(BF16)


def pack_kernel(tables, rows, side_ref, conv_ref, bias_ref, reg_ref, first_ref, last_ref, *refs):
    ch = conv_ref.shape[1]
    weight_refs = refs[: len(tables)]
    (
        wide_ref, inner_ref, outer_ref, edges_ref, turn_ref, first_rows_ref, last_rows_ref,
        line_ref, sparse_ref,
    ) = refs[len(tables) :]
    pick = pick_rows(side_ref[0], ch * rows, rows)
    for plane_ref, rows_ref in ((first_ref, first_rows_ref), (last_ref, last_rows_ref)):
        x = plane_ref[...].reshape(ch * rows, plane_ref.shape[2])
        y = jnp.dot(pick, x, preferred_element_type=F32)
        rows_ref[...] = y.astype(BF16).reshape(rows_ref.shape)
    for table, out_ref in zip(tables, weight_refs):
        for m, row in enumerate(table):
            for k, t in enumerate(row):
                block = jnp.zeros((ch, ch), BF16) if t is None else conv_ref[t]
                out_ref[m * ch : (m + 1) * ch, k * ch : (k + 1) * ch] = block
    wide_ref[...] = jnp.broadcast_to(bias_ref[...], wide_ref.shape)
    size = turn_ref.shape[0]
    r = lax.broadcasted_iota(jnp.int32, (size, size), 0)
    k = lax.broadcasted_iota(jnp.int32, (size, size), 1)
    half = size // rows
    hit = k == (r % half) * rows + r // half
    turn_ref[...] = jnp.where(hit, 1.0, 0.0).astype(BF16)

    reg = reg_ref[...].astype(F32)
    line_ref[...] = jnp.zeros_like(line_ref)
    sparse_ref[...] = jnp.zeros_like(sparse_ref)
    for a in range(3):
        for b in range(3):
            for c in range(3):
                t = tap(a, b, c)
                one = reg[t : t + 1]
                line_ref[a * 3 + c : a * 3 + c + 1, b * ch : (b + 1) * ch] = one
                for p in range(2):
                    q = p + 2 - a
                    for e in range(2):
                        at = q * 24 + c * 6 + (2 - b) + 3 * e
                        col = (2 * p + e) * ch
                        sparse_ref[at : at + 1, col : col + ch] = one
    edges_ref[...] = sparse_ref[...].astype(BF16)
    width = line_ref.shape[1]
    row = lax.broadcasted_iota(jnp.int32, (rows, width), 0)
    for k in range(9):
        x = jnp.broadcast_to(line_ref[k : k + 1], (rows, width))
        step = 1
        while step < rows:
            x = jnp.where((row & step) != 0, pltpu.roll(x, step * ch, 1), x)
            step *= 2
        at = slice(k * rows, (k + 1) * rows)
        outer_ref[at] = x[:, : (rows + 2) * ch].astype(BF16)
        inner_ref[at] = pltpu.roll(x, width - ch, 1)[:, : rows * ch].astype(BF16)


def packed(side, conv_weight, conv_bias, reg_weight, first, last):
    rows, width = first.shape[1:]
    ch = conv_weight.shape[1]
    tables = [spread_table(), halo_table(0), halo_table(2), single_table()]
    shapes = [((len(t) * ch, len(t[0]) * ch), BF16) for t in tables]
    shapes += [
        ((ch, width), F32), ((9 * rows, rows * ch), BF16), ((9 * rows, (rows + 2) * ch), BF16),
        ((96, 4 * ch), BF16), ((rows * ch // 2, rows * ch // 2), BF16),
        ((2, ch, width), BF16), ((2, ch, width), BF16),
    ]
    outs = [jax.ShapeDtypeStruct(*x) for x in shapes]
    line = -(-(rows + 3) * ch // 128) * 128
    args = conv_weight, conv_bias[:, None], reg_weight, first, last
    return pl.pallas_call(
        functools.partial(pack_kernel, tables, rows),
        name="pack",
        grid=(1,),
        out_shape=outs,
        in_specs=[SMEM, *map(whole, args)],
        out_specs=[whole(x) for x in outs],
        scratch_shapes=[pltpu.VMEM((16, line), F32), pltpu.VMEM((96, 4 * ch), F32)],
        compiler_params=ROOM,
    )(side, *args)


def shifted(x, by):
    width = x.shape[-1]
    moved = pltpu.roll(x, by % width, x.ndim - 1)
    lane = lax.broadcasted_iota(jnp.int32, x.shape[:-1] + (128,), x.ndim - 1)
    zero = jnp.zeros(x.shape[:-1] + (128,), x.dtype)
    if by == 1:
        edge = jnp.where(lane == 0, zero, moved[..., :128])
        return jnp.concatenate([edge, moved[..., 128:]], axis=-1)
    edge = jnp.where(lane == 127, zero, moved[..., width - 128 :])
    return jnp.concatenate([moved[..., : width - 128], edge], axis=-1)


def put(taps_ref, slot, row, at, x):
    count, size, width = x.shape
    ch = taps_ref.shape[2] // 3
    flat = x.reshape(count * size, width)
    for c, y in ((0, shifted(flat, 1)), (1, flat), (2, shifted(flat, -1))):
        taps_ref[slot, pl.ds(row, count), pl.ds(c * ch + at, size), :] = y.reshape(x.shape)


def turn(taps_ref, slot, row, at, block, turn_ref):
    size, rows, width = block.shape
    ch = taps_ref.shape[2] // 3
    y = jnp.dot(turn_ref[...], block.reshape(size * rows, width), preferred_element_type=F32)
    taps_ref[slot, pl.ds(row, rows), ch + at : ch + at + size, :] = (
        y.astype(BF16).reshape(rows, size, width)
    )


def spread(taps_ref, slot, row, count):
    width = taps_ref.shape[3]
    ch = taps_ref.shape[2] // 3
    x = taps_ref[slot, pl.ds(row, count), ch : 2 * ch, :].reshape(count * ch, width)
    taps_ref[slot, pl.ds(row, count), :ch, :] = shifted(x, 1).reshape(count, ch, width)
    taps_ref[slot, pl.ds(row, count), 2 * ch :, :] = shifted(x, -1).reshape(count, ch, width)


def inner_kernel(
    side_ref, vol_ref, weight_ref, bias_ref, reg_ref, turn_ref, cost_ref, pre_ref, near_ref,
    taps_ref, acc_ref, hidden_ref, sums_ref,
):
    s = pl.program_id(0)
    last = pl.num_programs(0) - 1
    ch, _, rows, width = vol_ref.shape
    planes = cost_ref.shape[0]
    half = ch // 2
    new = (s % 2) * 2
    old = ((s + 1) % 2) * 2

    def stage(part):
        p, h = part // 4, part % 4
        if h < 2:
            block = vol_ref[h * half : (h + 1) * half, p]
            turn(taps_ref, new + p, 0, h * half, block, turn_ref)
        else:
            spread(taps_ref, new + p, (h - 2) * (rows // 2), rows // 2)
        if h == 2:
            block = jnp.minimum(s, last - 1)
            near = jnp.where(side_ref[0] == 0, rows - 1, 0)
            near_ref[2 * block + p] = taps_ref[new + p, near, ch : 2 * ch, :]

            @pl.when((block == 0) | (block == last - 1))
            def _():
                far = jnp.where(side_ref[0] == 0, rows - 2, 1)
                at = planes + p + jnp.where(block == 0, 0, 2)
                near_ref[at] = taps_ref[new + p, far, ch : 2 * ch, :]

    @pl.when(s == 0)
    def _():
        for part in range(8):
            stage(part)
        sums_ref[...] = jnp.zeros_like(sums_ref)
        hidden_ref[...] = jnp.zeros_like(hidden_ref)

    @pl.when(s >= 1)
    def _():
        base = 2 * (s - 1) + 3
        tiles = rows // 2
        for p in range(2):
            slots = [(base + p + do) % 4 for do in range(3)]
            for j in range(tiles):
                ho0 = 1 if j == 0 else 0
                ho1 = 3 if j == tiles - 1 else 4
                w = weight_ref[ho0 * 3 * ch : ho1 * 3 * ch]
                x = taps_ref[old + p, 2 * j : 2 * j + 2].reshape(6 * ch, width)
                y = jnp.dot(w, x, preferred_element_type=F32)
                for ho in range(ho0, ho1):
                    for do in range(3):
                        at = ((ho - ho0) * 3 + do) * ch
                        part = y[at : at + ch]
                        fresh = do == 2 and (ho >= 2 or j == 0)
                        if not fresh:
                            part = part + acc_ref[slots[do], 2 * j + ho]
                        acc_ref[slots[do], 2 * j + ho] = part
                if (j + 1) * 4 // tiles > j * 4 // tiles:
                    stage(4 * p + j * 4 // tiles)

    @pl.when(s >= 2)
    def _():
        first = 2 * (s - 1) - 1
        for q in range(2):
            slot = (first + q) % 4
            pre_ref[q, 0] = acc_ref[slot, 1]
            pre_ref[q, 1] = acc_ref[slot, rows]
            for r in range(1, rows - 1):
                y = jnp.maximum(acc_ref[slot, r + 1] + bias_ref[...], 0.0)
                hidden_ref[q, r * ch : (r + 1) * ch, :] = y.astype(BF16)
            y = jnp.dot(reg_ref[...], hidden_ref[q], preferred_element_type=F32)
            for a in range(3):
                for c in range(3):
                    at = (a * 3 + c) * rows
                    sums_ref[c, first + q + 1 - a] += y[at : at + rows]

    @pl.when(s == last)
    def _():
        def finish(d, carry):
            cost_ref[d] = shifted(sums_ref[0, d], 1) + sums_ref[1, d] + shifted(sums_ref[2, d], -1)
            return carry

        lax.fori_loop(0, planes, finish, 0)


def inner(side, volume, weights, bias, reg, turning):
    ch, planes, rows, width = volume.shape
    blocks = planes // 2
    cost = jax.ShapeDtypeStruct((planes, rows, width), F32)
    pre = jax.ShapeDtypeStruct((planes - 2, 2, ch, width), F32)
    near = jax.ShapeDtypeStruct((planes + 4, ch, width), BF16)
    work = 2 * 27 * ch * ch * planes * rows * width
    return pl.pallas_call(
        inner_kernel,
        name="inner",
        grid=(blocks + 1,),
        out_shape=(cost, pre, near),
        in_specs=[
            SMEM,
            pl.BlockSpec((ch, 2, rows, width), lambda s: (0, jnp.minimum(s, blocks - 1), 0, 0)),
            whole(weights), whole(bias), whole(reg), whole(turning),
        ],
        out_specs=(
            whole(cost),
            pl.BlockSpec((2, 2, ch, width), lambda s: (jnp.maximum(s - 2, 0), 0, 0, 0)),
            whole(near),
        ),
        scratch_shapes=[
            pltpu.VMEM((4, rows, 3 * ch, width), BF16),
            pltpu.VMEM((4, rows + 2, ch, width), F32),
            pltpu.VMEM((2, rows * ch, width), BF16),
            pltpu.VMEM((3, planes, rows, width), F32),
        ],
        compiler_params=ROOM,
        cost_estimate=pl.CostEstimate(
            flops=2 * work, bytes_accessed=volume.size * 2, transcendentals=0
        ),
    )(side, volume, weights, bias, reg, turning)


def sides_kernel(
    side_ref, near_ref, pre_ref, above_ref, below_ref, bias_ref, reg_ref, out_ref, send_ref,
    taps_ref, acc_ref, hidden_ref, sums_ref,
):
    planes, _, width = out_ref.shape
    ch = near_ref.shape[1]
    side = side_ref[0]
    w = jnp.where(side == 0, below_ref[...], above_ref[...])
    e = 1 - side
    acc_ref[...] = jnp.zeros_like(acc_ref)
    sums_ref[...] = jnp.zeros_like(sums_ref)
    for d in range(planes):
        put(taps_ref, d // 2, d % 2, 0, near_ref[d][None])
    for k in range(planes // 2):
        x = taps_ref[k].reshape(6 * ch, width)
        y = jnp.dot(w, x, preferred_element_type=F32)
        for q in range(4):
            acc_ref[2 * k + q] += y[q * ch : (q + 1) * ch]
    for k in range(planes // 2 - 1):
        for p in range(2):
            d = 2 * k + 1 + p
            for row in range(2):
                y = pre_ref[d - 1, row] + jnp.where(e == row, acc_ref[d + 1], 0.0)
                y = jnp.maximum(y + bias_ref[...], 0.0).astype(BF16)
                hidden_ref[k, (2 * p + row) * ch : (2 * p + row + 1) * ch, :] = y
        y = jnp.dot(reg_ref[...], hidden_ref[k], preferred_element_type=F32)
        for q in range(4):
            sums_ref[2 * k + q] += y[q * 24 : (q + 1) * 24]
    for d in range(planes):
        y = sums_ref[d]
        right, left = shifted(y, 1), shifted(y, -1)
        total = right[0:6] + y[6:12] + left[12:18]
        out_ref[d, 0:6] = total
        send_ref[d : d + 1] = jnp.where(side == 0, total[5:6], total[0:1])


def sides(side, near, pre, above, below, bias, reg):
    ch, width = near.shape[1:]
    planes = near.shape[0] - 4
    args = near, pre, above, below, bias, reg
    outs = (
        jax.ShapeDtypeStruct((planes, 8, width), F32),
        jax.ShapeDtypeStruct((planes, width), F32),
    )
    return pl.pallas_call(
        sides_kernel,
        name="sides",
        grid=(1,),
        out_shape=outs,
        in_specs=[SMEM, *map(whole, args)],
        out_specs=[whole(x) for x in outs],
        scratch_shapes=[
            pltpu.VMEM((planes // 2, 2, 3 * ch, width), BF16),
            pltpu.VMEM((planes + 2, ch, width), F32),
            pltpu.VMEM((planes // 2 - 1, 4 * ch, width), BF16),
            pltpu.VMEM((planes, 24, width), F32),
        ],
        compiler_params=ROOM,
        cost_estimate=pl.CostEstimate(flops=1 << 31, bytes_accessed=1 << 22, transcendentals=0),
    )(side, *args)


def outer_kernel(
    side_ref, vol_ref, near_ref, lo_ref, hi_ref, lo_rows_ref, hi_rows_ref, weight_ref, bias_ref,
    reg_ref, turn_ref, out_ref, taps_ref, hidden_ref,
):
    s = pl.program_id(0)
    ch, _, rows, width = vol_ref.shape
    planes = near_ref.shape[0] - 4
    half = ch // 2
    above = side_ref[0] == 1

    def stage_rows(slot, near, far):
        zero = jnp.zeros_like(near)
        put(taps_ref, slot, 0, 0, jnp.where(above, far, zero)[None])
        put(taps_ref, slot, 1, 0, jnp.where(above, near, zero)[None])
        put(taps_ref, slot, rows + 2, 0, jnp.where(above, zero, near)[None])
        put(taps_ref, slot, rows + 3, 0, jnp.where(above, zero, far)[None])

    low = s == 0
    for p in range(2):
        stage_rows(1 + p - s, near_ref[s * (planes - 2) + p], near_ref[planes + 2 * s + p])
    corner = jnp.where(low, lo_rows_ref[...], hi_rows_ref[...])
    stage_rows(2 * s, corner[0], corner[1])
    for h in range(2):
        part = slice(h * half, (h + 1) * half)
        for p in range(2):
            turn(taps_ref, 1 + p - s, 2, h * half, vol_ref[part, p], turn_ref)
        far_block = jnp.where(low, lo_ref[part], hi_ref[part])
        turn(taps_ref, 2 * s, 2, h * half, far_block, turn_ref)
    for slot in range(3):
        for r in range(0, rows, rows // 2):
            spread(taps_ref, slot, 2 + r, rows // 2)

    for j in range(rows // 2 + 1):
        sums = {}
        at = 0
        for blocks, outs in SINGLE:
            pieces = [taps_ref[dd, 2 * j + hh, c0 * ch : c1 * ch] for dd, hh, c0, c1 in blocks]
            x = jnp.concatenate(pieces, axis=0)
            w = weight_ref[at : at + len(outs) * ch, : x.shape[0]]
            y = jnp.dot(w, x, preferred_element_type=F32)
            for k, ho in enumerate(outs):
                part = y[k * ch : (k + 1) * ch]
                sums[ho] = sums[ho] + part if ho in sums else part
            at += len(outs) * ch
        for ho, y in sums.items():
            y = jnp.maximum(y + bias_ref[...], 0.0)
            r = 2 * j + ho
            if r == 0:
                y = jnp.where(above, y, 0.0)
            if r == rows + 1:
                y = jnp.where(above, 0.0, y)
            hidden_ref[r * ch : (r + 1) * ch] = y.astype(BF16)
    y = jnp.dot(reg_ref[...], hidden_ref[...], preferred_element_type=F32)
    for a in range(3):
        r = [y[(a * 3 + c) * rows : (a * 3 + c + 1) * rows] for c in range(3)]
        out_ref[0, 2 - a] = shifted(r[0], 1) + r[1] + shifted(r[2], -1)


def outer(side, volume, near, halos, weights, bias, reg, turning):
    ch, planes, rows, width = volume.shape
    out = jax.ShapeDtypeStruct((2, 3, rows, width), F32)
    work = 2 * 27 * ch * ch * 2 * rows * width
    return pl.pallas_call(
        outer_kernel,
        name="outer",
        grid=(2,),
        out_shape=out,
        in_specs=[
            SMEM,
            pl.BlockSpec((ch, 2, rows, width), lambda s: (0, s * (planes // 2 - 1), 0, 0)),
            whole(near), *map(whole, halos), whole(weights), whole(bias), whole(reg),
            whole(turning),
        ],
        out_specs=pl.BlockSpec((1, 3, rows, width), lambda s: (s, 0, 0, 0)),
        scratch_shapes=[
            pltpu.VMEM((3, rows + 4, 3 * ch, width), BF16),
            pltpu.VMEM(((rows + 2) * ch, width), BF16),
        ],
        compiler_params=ROOM,
        cost_estimate=pl.CostEstimate(flops=2 * work, bytes_accessed=1 << 22, transcendentals=0),
    )(side, volume, near, *halos, weights, bias, reg, turning)


def stats_kernel(
    first_ref, side_ref, cost_ref, sides_ref, row_ref, outer_ref, out_ref, score_ref
):
    planes, rows, width = cost_ref.shape
    row = lax.broadcasted_iota(jnp.int32, (rows, width), 0)
    mine = jnp.where(side_ref[0] == 1, 0, rows - 1)

    def cost_of(d):
        cost = cost_ref[d]
        for k, r in ((1, 0), (2, 1), (3, rows - 2), (4, rows - 1)):
            cost = cost + jnp.where(row == r, sides_ref[d, k : k + 1], 0.0)
        return cost + jnp.where(row == mine, row_ref[d : d + 1], 0.0)

    extra = {0: outer_ref[0, 1], 1: outer_ref[0, 2]}
    for d, x in ((planes - 2, outer_ref[1, 0]), (planes - 1, outer_ref[1, 1])):
        extra[d] = x if d not in extra else extra[d] + x
    peak = None
    for d in range(1, planes - 1):
        cost = cost_of(d)
        if d in extra:
            cost = cost + extra[d]
        score = -cost
        score_ref[d] = score
        peak = score if peak is None else jnp.maximum(peak, score)
    total = jnp.zeros((rows, width), F32)
    moment = jnp.zeros((rows, width), F32)
    first = first_ref[0].astype(F32)
    for d in range(1, planes - 1):
        expo = jnp.exp(score_ref[d] - peak)
        total = total + expo
        moment = moment + (first + float(d)) * expo
    values = (
        peak, total, moment, cost_of(0) + extra[0], cost_of(planes - 1) + extra[planes - 1],
        outer_ref[0, 0], outer_ref[1, 2], jnp.zeros((rows, width), F32),
    )
    for k, value in enumerate(values):
        for t in range(rows // 8):
            for u in range(width // 128):
                tile = value[t * 8 : (t + 1) * 8, u * 128 : (u + 1) * 128]
                out_ref[t * (width // 128) + u, k] = tile


def stats(first, side, cost, sides_cost, row, outer_cost):
    planes, rows, width = cost.shape
    args = cost, sides_cost, row, outer_cost
    out = jax.ShapeDtypeStruct((rows * width // 1024, 8, 8, 128), F32)
    return pl.pallas_call(
        stats_kernel,
        name="stats",
        grid=(1,),
        out_shape=out,
        in_specs=[SMEM, SMEM, *map(whole, args)],
        out_specs=whole(out),
        scratch_shapes=[pltpu.VMEM((planes, rows, width), F32)],
        compiler_params=ROOM,
    )(first, side, *args)


def join_kernel(planes, in_ref, out_ref):
    count = in_ref.shape[0]
    scores = []
    peak = None
    for j in range(count):
        low, high = in_ref[j, 3], in_ref[j, 4]
        if j > 0:
            low = low + in_ref[j - 1, 6]
        if j < count - 1:
            high = high + in_ref[j + 1, 5]
        scores.append((-low, -high))
        here = jnp.maximum(in_ref[j, 0], jnp.maximum(-low, -high))
        peak = here if peak is None else jnp.maximum(peak, here)
    total = jnp.zeros_like(peak)
    moment = jnp.zeros_like(peak)
    for j in range(count):
        scale = jnp.exp(in_ref[j, 0] - peak)
        low, high = (jnp.exp(score - peak) for score in scores[j])
        total = total + in_ref[j, 1] * scale + low + high
        ends = float(j * planes) * low + float((j + 1) * planes - 1) * high
        moment = moment + in_ref[j, 2] * scale + ends
    result = moment / total
    for j in range(count):
        out_ref[j] = result


def join(pieces, planes):
    count, _, rows, width = pieces.shape
    out = jax.ShapeDtypeStruct((count, rows, width), F32)
    return pl.pallas_call(
        functools.partial(join_kernel, planes),
        name="join",
        grid=(1,),
        out_shape=out,
        in_specs=[whole(pieces)],
        out_specs=whole(out),
        compiler_params=ROOM,
    )(pieces)


def joined(values, planes, rows, width):
    count = lax.axis_size("disp")
    tiles = values.shape[0]
    if count > tiles:
        parts = count // tiles
        values = values.reshape(tiles, 8, parts, 8 // parts, 128)
        values = jnp.swapaxes(values, 1, 2).reshape(count, 8, 8 // parts, 128)
    elif count < tiles:
        parts = tiles // count
        values = values.reshape(count, parts, 8, 8, 128)
        values = jnp.swapaxes(values, 1, 2).reshape(count, 8, parts * 8, 128)
    pieces = lax.all_to_all(values, "disp", 0, 0)
    result = lax.all_to_all(join(pieces, planes), "disp", 0, 0)
    result = result.reshape(rows // 8, width // 128, 8, 128)
    return jnp.swapaxes(result, 1, 2).reshape(rows, width)


def exchange(x, axis):
    return lax.ppermute(x, axis, [(0, 1), (1, 0)] if lax.axis_size(axis) == 2 else [])


def up(x, axis):
    count = lax.axis_size(axis)
    return lax.ppermute(x, axis, [(i, i + 1) for i in range(count - 1)])


def down(x, axis):
    count = lax.axis_size(axis)
    return lax.ppermute(x, axis, [(i + 1, i) for i in range(count - 1)])


def across(x, step):
    count = lax.axis_size("disp")
    sides = lax.axis_size("rows")
    pairs = [
        (i * sides + r, (i + step) * sides + 1 - r)
        for i in range(count) for r in range(sides)
        if 0 <= i + step < count and sides == 2
    ]
    return lax.ppermute(x, ("disp", "rows"), pairs)


def body(volume, conv_weight, conv_bias, reg_weight):
    ch, planes, rows, width = volume.shape
    side = lax.axis_index("rows").astype(jnp.int32).reshape(1)
    first = (lax.axis_index("disp") * planes).astype(jnp.int32).reshape(1)

    ends = volume[:, planes - 1], volume[:, 0]
    volume, ends = lax.optimization_barrier((volume, ends))
    lo = up(ends[0], "disp")
    hi = down(ends[1], "disp")
    (
        spread_w, above, below, single, bias, reg_inner, reg_outer, reg_edges, turning,
        first_rows, last_rows,
    ) = packed(side, conv_weight, conv_bias, reg_weight, ends[1], ends[0])
    lo_rows = across(last_rows, 1)
    hi_rows = across(first_rows, -1)

    cost, pre, near = inner(side, volume, spread_w, bias, reg_inner, turning)
    near, lo, hi, lo_rows, hi_rows = lax.optimization_barrier((near, lo, hi, lo_rows, hi_rows))
    near = exchange(near, "rows")
    sides_cost, send = sides(side, near, pre, above, below, bias, reg_edges)
    row = exchange(send, "rows")
    halos = (lo, hi, lo_rows, hi_rows)
    outer_cost = outer(side, volume, near, halos, single, bias, reg_outer, turning)
    values = stats(first, side, cost, sides_cost, row, outer_cost)
    return joined(values, planes, rows, width)


def solution(mesh):
    in_specs = (P(None, "disp", ("tiles", "rows"), None), P(), P(), P())
    out_specs = P(("tiles", "rows"), None)
    return jax.shard_map(body, mesh=mesh, in_specs=in_specs, out_specs=out_specs, check_vma=False)
```

```python
import functools

import jax
import jax.numpy as jnp
import numpy as np
from jax import lax
from jax.experimental import pallas as pl
from jax.experimental.pallas import tpu as pltpu
from jax.sharding import PartitionSpec as P

BF16 = jnp.bfloat16
F32 = jnp.float32
SMEM = pl.BlockSpec(memory_space=pltpu.SMEM)
ROOM = pltpu.CompilerParams(vmem_limit_bytes=56 << 20)


def whole(x):
    return pl.BlockSpec(x.shape, lambda s: (0,) * x.ndim)

SINGLE = (
    (((0, 0, 0, 3), (1, 0, 0, 3), (2, 0, 0, 2)), (0,)),
    (((0, 3, 0, 3), (1, 3, 0, 3), (2, 3, 0, 2)), (1,)),
    (((0, 1, 0, 3), (0, 2, 0, 3), (1, 1, 0, 2)), (0, 1)),
    (((1, 1, 2, 3), (1, 2, 0, 3), (2, 1, 0, 3), (2, 2, 0, 1)), (0, 1)),
    (((2, 2, 1, 3), (2, 0, 2, 3), (2, 3, 2, 3)), (0, 1)),
)


def tap(a, b, c):
    return 9 * a + 3 * b + c if 0 <= a < 3 and 0 <= b < 3 else None


def single_table():
    table = []
    for blocks, outs in SINGLE:
        for ho in outs:
            row = [tap(dd, hh - ho, c) for dd, hh, c0, c1 in blocks for c in range(c0, c1)]
            table.append(row + [None] * (8 - len(row)))
    return table


def table_of(tiles):
    table = []
    for blocks, outs in tiles:
        for do, ho in outs:
            table.append(
                [tap(dd - do, hh - ho, c) for dd, hh, c0, c1 in blocks for c in range(c0, c1)]
            )
    return table


CENTER = (
    (
        ((1, 1, 0, 3), (1, 2, 0, 3), (0, 0, 2, 3), (0, 3, 2, 3))
        + ((2, 1, 0, 3), (2, 2, 0, 3), (3, 3, 2, 3), (3, 0, 2, 3)),
        ((0, 0), (0, 1), (1, 0), (1, 1)),
    ),
)
RIM = (
    (((0, 1, 0, 3), (0, 2, 0, 3), (0, 0, 0, 2)), ((0, 0), (0, 1))),
    (((3, 1, 0, 3), (3, 2, 0, 3), (3, 3, 0, 2)), ((1, 0), (1, 1))),
    (((1, 0, 0, 3), (2, 0, 0, 3), (3, 0, 0, 2)), ((0, 0), (1, 0))),
    (((1, 3, 0, 3), (2, 3, 0, 3), (0, 3, 0, 2)), ((0, 1), (1, 1))),
)


def side_tiles(out):
    first, second = (0, out), (1, out)
    return (
        (
            ((1, 0, 0, 3), (1, 1, 0, 3), (0, 0, 0, 2))
            + ((2, 0, 0, 3), (2, 1, 0, 3), (3, 0, 0, 2))
            + ((0, 0, 2, 3), (0, 1, 0, 3), (3, 0, 2, 3), (3, 1, 0, 3)),
            (first, second),
        ),
    )


def halo_table(b):
    return [[tap(p - q + 2, b, c) for p in range(2) for c in range(3)] for q in range(4)]


def pick_rows(side, width, rows):
    ch = width // rows
    r = lax.broadcasted_iota(jnp.int32, (2 * ch, width), 0)
    k = lax.broadcasted_iota(jnp.int32, (2 * ch, width), 1)
    far = jnp.where(r >= ch, 1, 0)
    row = jnp.where(side == 0, rows - 1 - far, far)
    return jnp.where(k == (r - ch * far) * rows + row, 1.0, 0.0).astype(BF16)


def pack_kernel(tables, rows, side_ref, conv_ref, bias_ref, reg_ref, first_ref, last_ref, *refs):
    ch = conv_ref.shape[1]
    weight_refs = refs[: len(tables)]
    (
        wide_ref, inner_ref, outer_ref, edges_ref, turn_ref, first_rows_ref, last_rows_ref,
        line_ref, sparse_ref,
    ) = refs[len(tables) :]
    pick = pick_rows(side_ref[0], ch * rows, rows)
    for plane_ref, rows_ref in ((first_ref, first_rows_ref), (last_ref, last_rows_ref)):
        x = plane_ref[...].reshape(ch * rows, plane_ref.shape[2])
        y = jnp.dot(pick, x, preferred_element_type=F32)
        rows_ref[...] = y.astype(BF16).reshape(rows_ref.shape)
    for table, out_ref in zip(tables, weight_refs):
        for m, row in enumerate(table):
            for k, t in enumerate(row):
                block = jnp.zeros((ch, ch), BF16) if t is None else conv_ref[t]
                out_ref[m * ch : (m + 1) * ch, k * ch : (k + 1) * ch] = block
    wide_ref[...] = jnp.broadcast_to(bias_ref[...], wide_ref.shape)
    size = turn_ref.shape[0]
    r = lax.broadcasted_iota(jnp.int32, (size, size), 0)
    k = lax.broadcasted_iota(jnp.int32, (size, size), 1)
    half = size // rows
    hit = k == (r % half) * rows + r // half
    turn_ref[...] = jnp.where(hit, 1.0, 0.0).astype(BF16)

    reg = reg_ref[...].astype(F32)
    line_ref[...] = jnp.zeros_like(line_ref)
    sparse_ref[...] = jnp.zeros_like(sparse_ref)
    for a in range(3):
        for b in range(3):
            for c in range(3):
                t = tap(a, b, c)
                one = reg[t : t + 1]
                line_ref[a * 3 + c : a * 3 + c + 1, b * ch : (b + 1) * ch] = one
                for p in range(2):
                    q = p + 2 - a
                    for e in range(2):
                        at = q * 24 + c * 6 + (2 - b) + 3 * e
                        col = (2 * p + e) * ch
                        sparse_ref[at : at + 1, col : col + ch] = one
    edges_ref[...] = sparse_ref[...].astype(BF16)
    width = line_ref.shape[1]
    row = lax.broadcasted_iota(jnp.int32, (rows, width), 0)
    for k in range(9):
        x = jnp.broadcast_to(line_ref[k : k + 1], (rows, width))
        step = 1
        while step < rows:
            x = jnp.where((row & step) != 0, pltpu.roll(x, step * ch, 1), x)
            step *= 2
        at = slice(k * rows, (k + 1) * rows)
        outer_ref[at] = x[:, : (rows + 2) * ch].astype(BF16)
        inner_ref[at] = pltpu.roll(x, width - ch, 1)[:, : rows * ch].astype(BF16)


def packed(side, conv_weight, conv_bias, reg_weight, first, last):
    rows, width = first.shape[1:]
    ch = conv_weight.shape[1]
    tables = [table_of(CENTER), table_of(RIM), table_of(side_tiles(-1)), table_of(side_tiles(0))]
    tables += [halo_table(0), halo_table(2), single_table()]
    shapes = [((len(t) * ch, len(t[0]) * ch), BF16) for t in tables]
    shapes += [
        ((ch, width), F32), ((9 * rows, rows * ch), BF16), ((9 * rows, (rows + 2) * ch), BF16),
        ((96, 4 * ch), BF16), ((rows * ch // 2, rows * ch // 2), BF16),
        ((2, ch, width), BF16), ((2, ch, width), BF16),
    ]
    outs = [jax.ShapeDtypeStruct(*x) for x in shapes]
    line = -(-(rows + 3) * ch // 128) * 128
    args = conv_weight, conv_bias[:, None], reg_weight, first, last
    return pl.pallas_call(
        functools.partial(pack_kernel, tables, rows),
        name="pack",
        grid=(1,),
        out_shape=outs,
        in_specs=[SMEM, *map(whole, args)],
        out_specs=[whole(x) for x in outs],
        scratch_shapes=[pltpu.VMEM((16, line), F32), pltpu.VMEM((96, 4 * ch), F32)],
        compiler_params=ROOM,
    )(side, *args)


def shifted(x, by):
    width = x.shape[-1]
    moved = pltpu.roll(x, by % width, x.ndim - 1)
    lane = lax.broadcasted_iota(jnp.int32, x.shape[:-1] + (128,), x.ndim - 1)
    zero = jnp.zeros(x.shape[:-1] + (128,), x.dtype)
    if by == 1:
        edge = jnp.where(lane == 0, zero, moved[..., :128])
        return jnp.concatenate([edge, moved[..., 128:]], axis=-1)
    edge = jnp.where(lane == 127, zero, moved[..., width - 128 :])
    return jnp.concatenate([moved[..., : width - 128], edge], axis=-1)


def put(taps_ref, slot, row, at, x):
    count, size, width = x.shape
    ch = taps_ref.shape[2] // 3
    flat = x.reshape(count * size, width)
    for c, y in ((0, shifted(flat, 1)), (1, flat), (2, shifted(flat, -1))):
        taps_ref[slot, pl.ds(row, count), pl.ds(c * ch + at, size), :] = y.reshape(x.shape)


def turn(taps_ref, slot, row, at, block, turn_ref):
    size, rows, width = block.shape
    ch = taps_ref.shape[2] // 3
    y = jnp.dot(turn_ref[...], block.reshape(size * rows, width), preferred_element_type=F32)
    taps_ref[slot, pl.ds(row, rows), ch + at : ch + at + size, :] = (
        y.astype(BF16).reshape(rows, size, width)
    )


def spread(taps_ref, slot, row, count):
    width = taps_ref.shape[3]
    ch = taps_ref.shape[2] // 3
    x = taps_ref[slot, pl.ds(row, count), ch : 2 * ch, :].reshape(count * ch, width)
    taps_ref[slot, pl.ds(row, count), :ch, :] = shifted(x, 1).reshape(count, ch, width)
    taps_ref[slot, pl.ds(row, count), 2 * ch :, :] = shifted(x, -1).reshape(count, ch, width)


def inner_kernel(
    side_ref, vol_ref, center_ref, rim_ref, top_ref, bottom_ref, bias_ref, reg_ref, turn_ref,
    cost_ref, pre_ref, near_ref, taps0, taps1, taps2, hidden0, hidden1, hidden2, sums_ref,
):
    taps = taps0, taps1, taps2
    hidden = hidden0, hidden1, hidden2
    s = pl.program_id(0)
    ch, _, rows, width = vol_ref.shape
    planes = cost_ref.shape[0]
    blocks = planes // 2
    half = ch // 2

    def stage(new, part):
        p, h = part // 4, part % 4
        if h < 2:
            turn(new, p, 0, h * half, vol_ref[h * half : (h + 1) * half, p], turn_ref)
        else:
            spread(new, p, (h - 2) * (rows // 2), rows // 2)
        if h == 2:
            block = jnp.minimum(s, blocks - 1)
            near = jnp.where(side_ref[0] == 0, rows - 1, 0)
            near_ref[2 * block + p] = new[p, near, ch : 2 * ch, :]

            @pl.when((block == 0) | (block == blocks - 1))
            def _():
                far = jnp.where(side_ref[0] == 0, rows - 2, 1)
                at = planes + p + jnp.where(block == 0, 0, 2)
                near_ref[at] = new[p, far, ch : 2 * ch, :]

    def patch(old, mid, row, groups):
        sums = {}
        four = (old, 0), (old, 1), (mid, 0), (mid, 1)
        for tiles, w_ref in groups:
            at = 0
            for parts, outs in tiles:
                pieces = []
                for dd, hh, c0, c1 in parts:
                    ref, p = four[dd]
                    pieces.append(ref[p, row + hh, c0 * ch : c1 * ch, :])
                x = jnp.concatenate(pieces, axis=0)
                w = w_ref[at : at + len(outs) * ch]
                y = jnp.dot(w, x, preferred_element_type=F32)
                for k, out in enumerate(outs):
                    part = y[k * ch : (k + 1) * ch]
                    sums[out] = sums[out] + part if out in sums else part
                at += len(outs) * ch
        return sums

    def regress(old, q):
        first = 2 * (s - 3) + 1
        y = jnp.dot(reg_ref[...], old[q], preferred_element_type=F32)
        for a in range(3):
            for c in range(3):
                at = (a * 3 + c) * rows
                sums_ref[c, first + q + 3 - a] += y[at : at + rows]

    @pl.when(s == 0)
    def _():
        for part in range(8):
            stage(taps0, part)
        sums_ref[...] = jnp.zeros_like(sums_ref)
        for ref in hidden:
            ref[...] = jnp.zeros_like(ref)

    @pl.when(s == 1)
    def _():
        for part in range(8):
            stage(taps1, part)

    for r in range(3):
        @pl.when((s >= 2) & (s <= blocks) & (s % 3 == r))
        def _(r=r):
            new, mid, old = taps[r], taps[(r + 2) % 3], taps[(r + 1) % 3]
            hidden_new, hidden_old = hidden[r], hidden[(r + 2) % 3]
            patches = rows // 2 - 1
            part = 0
            for j in range(patches):
                sums = patch(old, mid, 2 * j, ((CENTER, center_ref), (RIM, rim_ref)))
                for (do, ho), y in sums.items():
                    at = (2 * j + 1 + ho) * ch
                    y = jnp.maximum(y + bias_ref[...], 0.0).astype(BF16)
                    hidden_new[do, at : at + ch, :] = y
                while part * patches < 8 * (j + 1) and part < 8:
                    stage(new, part)
                    part += 1
                if j in (1, 2):
                    regress(hidden_old, j - 1)
            for e, (row, w_ref) in enumerate(((0, top_ref), (rows - 2, bottom_ref))):
                for (do, _), y in patch(old, mid, row, ((side_tiles(e - 1), w_ref),)).items():
                    pre_ref[do, e] = y

    @pl.when(s == blocks + 1)
    def _():
        for q in range(2):
            regress(hidden[blocks % 3], q)

        def finish(d, carry):
            right, left = shifted(sums_ref[0, d + 2], 1), shifted(sums_ref[2, d + 2], -1)
            cost_ref[d] = right + sums_ref[1, d + 2] + left
            return carry

        lax.fori_loop(0, planes, finish, 0)


def inner(side, volume, *rest):
    ch, planes, rows, width = volume.shape
    blocks = planes // 2
    cost = jax.ShapeDtypeStruct((planes, rows, width), F32)
    pre = jax.ShapeDtypeStruct((planes - 2, 2, ch, width), F32)
    near = jax.ShapeDtypeStruct((planes + 4, ch, width), BF16)
    work = 2 * 27 * ch * ch * planes * rows * width
    return pl.pallas_call(
        inner_kernel,
        name="inner",
        grid=(blocks + 2,),
        out_shape=(cost, pre, near),
        in_specs=[
            SMEM,
            pl.BlockSpec((ch, 2, rows, width), lambda s: (0, jnp.minimum(s, blocks - 1), 0, 0)),
            *map(whole, rest),
        ],
        out_specs=(
            whole(cost),
            pl.BlockSpec(
                (2, 2, ch, width), lambda s: (jnp.clip(s - 2, 0, blocks - 2), 0, 0, 0)
            ),
            whole(near),
        ),
        scratch_shapes=[pltpu.VMEM((2, rows, 3 * ch, width), BF16)] * 3
        + [pltpu.VMEM((2, rows * ch, width), BF16)] * 3
        + [pltpu.VMEM((3, planes + 4, rows, width), F32)],
        compiler_params=ROOM,
        cost_estimate=pl.CostEstimate(
            flops=2 * work, bytes_accessed=volume.size * 2, transcendentals=0
        ),
    )(side, volume, *rest)


def sides_kernel(
    side_ref, near_ref, pre_ref, above_ref, below_ref, bias_ref, reg_ref, out_ref, send_ref,
    taps_ref, acc_ref, hidden_ref, sums_ref,
):
    planes, _, width = out_ref.shape
    ch = near_ref.shape[1]
    side = side_ref[0]
    w = jnp.where(side == 0, below_ref[...], above_ref[...])
    e = 1 - side
    acc_ref[...] = jnp.zeros_like(acc_ref)
    sums_ref[...] = jnp.zeros_like(sums_ref)
    for d in range(planes):
        put(taps_ref, d // 2, d % 2, 0, near_ref[d][None])
    for k in range(planes // 2):
        x = taps_ref[k].reshape(6 * ch, width)
        y = jnp.dot(w, x, preferred_element_type=F32)
        for q in range(4):
            acc_ref[2 * k + q] += y[q * ch : (q + 1) * ch]
    for k in range(planes // 2 - 1):
        for p in range(2):
            d = 2 * k + 1 + p
            for row in range(2):
                y = pre_ref[d - 1, row] + jnp.where(e == row, acc_ref[d + 1], 0.0)
                y = jnp.maximum(y + bias_ref[...], 0.0).astype(BF16)
                hidden_ref[k, (2 * p + row) * ch : (2 * p + row + 1) * ch, :] = y
        y = jnp.dot(reg_ref[...], hidden_ref[k], preferred_element_type=F32)
        for q in range(4):
            sums_ref[2 * k + q] += y[q * 24 : (q + 1) * 24]
    for d in range(planes):
        y = sums_ref[d]
        right, left = shifted(y, 1), shifted(y, -1)
        total = right[0:6] + y[6:12] + left[12:18]
        out_ref[d, 0:6] = total
        send_ref[d : d + 1] = jnp.where(side == 0, total[5:6], total[0:1])


def sides(side, near, pre, above, below, bias, reg):
    ch, width = near.shape[1:]
    planes = near.shape[0] - 4
    args = near, pre, above, below, bias, reg
    outs = (
        jax.ShapeDtypeStruct((planes, 8, width), F32),
        jax.ShapeDtypeStruct((planes, width), F32),
    )
    return pl.pallas_call(
        sides_kernel,
        name="sides",
        grid=(1,),
        out_shape=outs,
        in_specs=[SMEM, *map(whole, args)],
        out_specs=[whole(x) for x in outs],
        scratch_shapes=[
            pltpu.VMEM((planes // 2, 2, 3 * ch, width), BF16),
            pltpu.VMEM((planes + 2, ch, width), F32),
            pltpu.VMEM((planes // 2 - 1, 4 * ch, width), BF16),
            pltpu.VMEM((planes, 24, width), F32),
        ],
        compiler_params=ROOM,
        cost_estimate=pl.CostEstimate(flops=1 << 31, bytes_accessed=1 << 22, transcendentals=0),
    )(side, *args)


def outer_kernel(
    side_ref, vol_ref, near_ref, lo_ref, hi_ref, lo_rows_ref, hi_rows_ref, weight_ref, bias_ref,
    reg_ref, turn_ref, out_ref, taps_ref, hidden_ref,
):
    s = pl.program_id(0)
    ch, _, rows, width = vol_ref.shape
    planes = near_ref.shape[0] - 4
    half = ch // 2
    above = side_ref[0] == 1

    def stage_rows(slot, near, far):
        zero = jnp.zeros_like(near)
        put(taps_ref, slot, 0, 0, jnp.where(above, far, zero)[None])
        put(taps_ref, slot, 1, 0, jnp.where(above, near, zero)[None])
        put(taps_ref, slot, rows + 2, 0, jnp.where(above, zero, near)[None])
        put(taps_ref, slot, rows + 3, 0, jnp.where(above, zero, far)[None])

    low = s == 0
    for p in range(2):
        stage_rows(1 + p - s, near_ref[s * (planes - 2) + p], near_ref[planes + 2 * s + p])
    corner = jnp.where(low, lo_rows_ref[...], hi_rows_ref[...])
    stage_rows(2 * s, corner[0], corner[1])
    for h in range(2):
        part = slice(h * half, (h + 1) * half)
        for p in range(2):
            turn(taps_ref, 1 + p - s, 2, h * half, vol_ref[part, p], turn_ref)
        far_block = jnp.where(low, lo_ref[part], hi_ref[part])
        turn(taps_ref, 2 * s, 2, h * half, far_block, turn_ref)
    for slot in range(3):
        for r in range(0, rows, rows // 2):
            spread(taps_ref, slot, 2 + r, rows // 2)

    for j in range(rows // 2 + 1):
        sums = {}
        at = 0
        for blocks, outs in SINGLE:
            pieces = [taps_ref[dd, 2 * j + hh, c0 * ch : c1 * ch] for dd, hh, c0, c1 in blocks]
            x = jnp.concatenate(pieces, axis=0)
            w = weight_ref[at : at + len(outs) * ch, : x.shape[0]]
            y = jnp.dot(w, x, preferred_element_type=F32)
            for k, ho in enumerate(outs):
                part = y[k * ch : (k + 1) * ch]
                sums[ho] = sums[ho] + part if ho in sums else part
            at += len(outs) * ch
        for ho, y in sums.items():
            y = jnp.maximum(y + bias_ref[...], 0.0)
            r = 2 * j + ho
            if r == 0:
                y = jnp.where(above, y, 0.0)
            if r == rows + 1:
                y = jnp.where(above, 0.0, y)
            hidden_ref[r * ch : (r + 1) * ch] = y.astype(BF16)
    y = jnp.dot(reg_ref[...], hidden_ref[...], preferred_element_type=F32)
    for a in range(3):
        r = [y[(a * 3 + c) * rows : (a * 3 + c + 1) * rows] for c in range(3)]
        out_ref[0, 2 - a] = shifted(r[0], 1) + r[1] + shifted(r[2], -1)


def outer(side, volume, near, halos, weights, bias, reg, turning):
    ch, planes, rows, width = volume.shape
    out = jax.ShapeDtypeStruct((2, 3, rows, width), F32)
    work = 2 * 27 * ch * ch * 2 * rows * width
    return pl.pallas_call(
        outer_kernel,
        name="outer",
        grid=(2,),
        out_shape=out,
        in_specs=[
            SMEM,
            pl.BlockSpec((ch, 2, rows, width), lambda s: (0, s * (planes // 2 - 1), 0, 0)),
            whole(near), *map(whole, halos), whole(weights), whole(bias), whole(reg),
            whole(turning),
        ],
        out_specs=pl.BlockSpec((1, 3, rows, width), lambda s: (s, 0, 0, 0)),
        scratch_shapes=[
            pltpu.VMEM((3, rows + 4, 3 * ch, width), BF16),
            pltpu.VMEM(((rows + 2) * ch, width), BF16),
        ],
        compiler_params=ROOM,
        cost_estimate=pl.CostEstimate(flops=2 * work, bytes_accessed=1 << 22, transcendentals=0),
    )(side, volume, near, *halos, weights, bias, reg, turning)


def stats_kernel(
    first_ref, side_ref, cost_ref, sides_ref, row_ref, outer_ref, out_ref, score_ref
):
    planes, rows, width = cost_ref.shape
    row = lax.broadcasted_iota(jnp.int32, (rows, width), 0)
    mine = jnp.where(side_ref[0] == 1, 0, rows - 1)

    def cost_of(d):
        cost = cost_ref[d]
        for k, r in ((1, 0), (2, 1), (3, rows - 2), (4, rows - 1)):
            cost = cost + jnp.where(row == r, sides_ref[d, k : k + 1], 0.0)
        return cost + jnp.where(row == mine, row_ref[d : d + 1], 0.0)

    extra = {0: outer_ref[0, 1], 1: outer_ref[0, 2]}
    for d, x in ((planes - 2, outer_ref[1, 0]), (planes - 1, outer_ref[1, 1])):
        extra[d] = x if d not in extra else extra[d] + x
    peak = None
    for d in range(1, planes - 1):
        cost = cost_of(d)
        if d in extra:
            cost = cost + extra[d]
        score = -cost
        score_ref[d] = score
        peak = score if peak is None else jnp.maximum(peak, score)
    total = jnp.zeros((rows, width), F32)
    moment = jnp.zeros((rows, width), F32)
    first = first_ref[0].astype(F32)
    for d in range(1, planes - 1):
        expo = jnp.exp(score_ref[d] - peak)
        total = total + expo
        moment = moment + (first + float(d)) * expo
    values = (
        peak, total, moment, cost_of(0) + extra[0], cost_of(planes - 1) + extra[planes - 1],
        outer_ref[0, 0], outer_ref[1, 2], jnp.zeros((rows, width), F32),
    )
    for k, value in enumerate(values):
        for t in range(rows // 8):
            for u in range(width // 128):
                tile = value[t * 8 : (t + 1) * 8, u * 128 : (u + 1) * 128]
                out_ref[t * (width // 128) + u, k] = tile


def stats(first, side, cost, sides_cost, row, outer_cost):
    planes, rows, width = cost.shape
    args = cost, sides_cost, row, outer_cost
    out = jax.ShapeDtypeStruct((rows * width // 1024, 8, 8, 128), F32)
    return pl.pallas_call(
        stats_kernel,
        name="stats",
        grid=(1,),
        out_shape=out,
        in_specs=[SMEM, SMEM, *map(whole, args)],
        out_specs=whole(out),
        scratch_shapes=[pltpu.VMEM((planes, rows, width), F32)],
        compiler_params=ROOM,
    )(first, side, *args)


def join_kernel(planes, in_ref, out_ref):
    count = in_ref.shape[0]
    scores = []
    peak = None
    for j in range(count):
        low, high = in_ref[j, 3], in_ref[j, 4]
        if j > 0:
            low = low + in_ref[j - 1, 6]
        if j < count - 1:
            high = high + in_ref[j + 1, 5]
        scores.append((-low, -high))
        here = jnp.maximum(in_ref[j, 0], jnp.maximum(-low, -high))
        peak = here if peak is None else jnp.maximum(peak, here)
    total = jnp.zeros_like(peak)
    moment = jnp.zeros_like(peak)
    for j in range(count):
        scale = jnp.exp(in_ref[j, 0] - peak)
        low, high = (jnp.exp(score - peak) for score in scores[j])
        total = total + in_ref[j, 1] * scale + low + high
        ends = float(j * planes) * low + float((j + 1) * planes - 1) * high
        moment = moment + in_ref[j, 2] * scale + ends
    result = moment / total
    for j in range(count):
        out_ref[j] = result


def join(pieces, planes):
    count, _, rows, width = pieces.shape
    out = jax.ShapeDtypeStruct((count, rows, width), F32)
    return pl.pallas_call(
        functools.partial(join_kernel, planes),
        name="join",
        grid=(1,),
        out_shape=out,
        in_specs=[whole(pieces)],
        out_specs=whole(out),
        compiler_params=ROOM,
    )(pieces)


def joined(values, planes, rows, width):
    count = lax.axis_size("disp")
    tiles = values.shape[0]
    if count > tiles:
        parts = count // tiles
        values = values.reshape(tiles, 8, parts, 8 // parts, 128)
        values = jnp.swapaxes(values, 1, 2).reshape(count, 8, 8 // parts, 128)
    elif count < tiles:
        parts = tiles // count
        values = values.reshape(count, parts, 8, 8, 128)
        values = jnp.swapaxes(values, 1, 2).reshape(count, 8, parts * 8, 128)
    pieces = lax.all_to_all(values, "disp", 0, 0)
    result = lax.all_to_all(join(pieces, planes), "disp", 0, 0)
    result = result.reshape(rows // 8, width // 128, 8, 128)
    return jnp.swapaxes(result, 1, 2).reshape(rows, width)


def exchange(x, axis):
    return lax.ppermute(x, axis, [(0, 1), (1, 0)] if lax.axis_size(axis) == 2 else [])


def up(x, axis):
    count = lax.axis_size(axis)
    return lax.ppermute(x, axis, [(i, i + 1) for i in range(count - 1)])


def down(x, axis):
    count = lax.axis_size(axis)
    return lax.ppermute(x, axis, [(i + 1, i) for i in range(count - 1)])


def across(x, step):
    count = lax.axis_size("disp")
    sides = lax.axis_size("rows")
    pairs = [
        (i * sides + r, (i + step) * sides + 1 - r)
        for i in range(count) for r in range(sides)
        if 0 <= i + step < count and sides == 2
    ]
    return lax.ppermute(x, ("disp", "rows"), pairs)


def body(volume, conv_weight, conv_bias, reg_weight):
    ch, planes, rows, width = volume.shape
    side = lax.axis_index("rows").astype(jnp.int32).reshape(1)
    first = (lax.axis_index("disp") * planes).astype(jnp.int32).reshape(1)

    ends = volume[:, planes - 1], volume[:, 0]
    volume, ends = lax.optimization_barrier((volume, ends))
    lo = up(ends[0], "disp")
    hi = down(ends[1], "disp")
    (
        center, rim, top, bottom, above, below, single, bias, reg_inner, reg_outer, reg_edges, turning,
        first_rows, last_rows,
    ) = packed(side, conv_weight, conv_bias, reg_weight, ends[1], ends[0])
    lo_rows = across(last_rows, 1)
    hi_rows = across(first_rows, -1)

    cost, pre, near = inner(
        side, volume, center, rim, top, bottom, bias, reg_inner, turning
    )
    near, lo, hi, lo_rows, hi_rows = lax.optimization_barrier((near, lo, hi, lo_rows, hi_rows))
    near = exchange(near, "rows")
    sides_cost, send = sides(side, near, pre, above, below, bias, reg_edges)
    row = exchange(send, "rows")
    halos = (lo, hi, lo_rows, hi_rows)
    outer_cost = outer(side, volume, near, halos, single, bias, reg_outer, turning)
    values = stats(first, side, cost, sides_cost, row, outer_cost)
    return joined(values, planes, rows, width)


def solution(mesh):
    in_specs = (P(None, "disp", ("tiles", "rows"), None), P(), P(), P())
    out_specs = P(("tiles", "rows"), None)
    return jax.shard_map(body, mesh=mesh, in_specs=in_specs, out_specs=out_specs, check_vma=False)
```
